128 devices in a mesh: rep: 8 (over y_lo, x), tp: 16 (over z, y_hi, core).
Axes of the slice: x: 4, y: 4 (y_hi: 2, y_lo: 2; y = y_hi * 2 + y_lo), z: 4, core: 2. Of those that a mesh axis runs over, the one named last changes fastest.
Arguments:
- hidden: bfloat16 [4, 1024, 8192], P(None, 'rep'), may hold values from -64 to 64
- norm_gain: bfloat16 [8192], replicated, may hold values from 0.099609375 to 1.8984375
- q_weight: bfloat16 [8192, 8192], P(('rep', 'tp')), may hold values from -0.0625 to 0.0625
- k_weight: bfloat16 [8192, 1024], P(('rep', 'tp')), may hold values from -0.0625 to 0.0625
- v_weight: bfloat16 [8192, 1024], P(('rep', 'tp')), may hold values from -0.0625 to 0.0625
- o_weight: bfloat16 [8192, 8192], P(('tp', 'rep')), may hold values from -0.0625 to 0.0625
- key_cache: bfloat16 [1024, 16, 192, 128], P('rep', 'tp'), may hold values from -256 to 256, as said below
- value_cache: bfloat16 [1024, 16, 192, 128], P('rep', 'tp'), may hold values from -8 to 8, as said below
- cache_len: int32 [1024], P('rep'), may hold values from 2 to 192
- finish: int32 [1024], P('rep'), may hold values from 0 to 4
- owner: int32 [1024, 1], P('rep'), may hold values from 0 to 127; in each aligned block of 128 rows (0 to 127, 128 to 255, ...) at most 2 rows name the same one
Outputs:
- decoded: bfloat16 [4, 1024, 8192], P(None, 'rep', 'tp')
- returned: bfloat16 [2048, 8192], P(('rep', 'tp'))
The draws below stay inside these ranges and needn't reach their ends.
Inputs may be any that keep to these rules, and one draw needn't show every extreme that they name: At most 2 rows of one replica, that is of one aligned block of 128 rows, have the same owner. `key_cache`: copies j = 0 to 1 of one key head are equal. `value_cache`: copies j = 0 to 1 of one value head are equal.
All inputs are finite; a program needn't handle non-finite values.
Results may differ from the reference program's by a relative error of at most 0.008.
Values may be sent and summed in bfloat16 or wider, within the bound.
A program may use at most 192 MiB of HBM per device.

```python
import math
import jax
import jax.numpy as jnp
import numpy as np
from jax import lax

D = 8192
HEADS = 64
KV = 8
HD = 128
ROWS_REP = 128
CACHE = 192
STEPS = 4
ROWS = 1024
DUP = 2
CAP = 2
N_REP = 8
N_TP = 16


def draw_hidden(key, part):
    key = jax.random.fold_in(key, 11)
    scale_key, base_key = jax.random.split(key, 2)
    scales = jnp.exp(jax.random.uniform(scale_key, (STEPS, ROWS, 1), jnp.float32, 0.0, math.log(10.0)))
    base = jnp.clip(jax.random.normal(base_key, (STEPS, ROWS, D), jnp.float32), -6.0, 6.0)
    values = base * scales
    return values.astype(jnp.bfloat16)


def draw_key_cache(key, part):
    key = jax.random.fold_in(key, 12)
    base_key = jax.random.fold_in(key, 0)
    base = jnp.clip(jax.random.normal(base_key, (ROWS, KV, 1, CACHE, HD), jnp.float32), -6.0, 6.0)
    copies = jnp.broadcast_to(base, (ROWS, KV, DUP, CACHE, HD)).reshape(ROWS, KV * DUP, CACHE, HD)
    return copies.astype(jnp.bfloat16)


def draw_value_cache(key, part):
    key = jax.random.fold_in(key, 13)
    base = jnp.clip(jax.random.normal(key, (ROWS, KV, 1, CACHE, HD), jnp.float32), -6.0, 6.0)
    copies = jnp.broadcast_to(base, (ROWS, KV, DUP, CACHE, HD)).reshape(ROWS, KV * DUP, CACHE, HD)
    return copies.astype(jnp.bfloat16)


def draw_cache_len(key, part):
    key = jax.random.fold_in(key, 14)
    length_key, pick_key = jax.random.split(key, 2)
    lengths = jax.random.randint(length_key, (ROWS,), 2, CACHE + 1, jnp.int32)
    picked = jax.random.randint(pick_key, (), 0, ROWS, jnp.int32)
    return jnp.where(jnp.arange(ROWS, dtype=jnp.int32) == picked, CACHE, lengths).astype(jnp.int32)


def set_ends(drawn, rng, smallest, largest):
    index_at = [jax.random.randint(jax.random.fold_in(rng, axis), (), 0, length) for axis, length in enumerate(drawn.shape)]
    widest = drawn.shape.index(max(drawn.shape))
    next_to = index_at[:widest] + [(index_at[widest] + 1) % drawn.shape[widest]] + index_at[widest + 1:]
    return drawn.at[tuple(index_at)].set(smallest).at[tuple(next_to)].set(largest)


def steps_of(stream_key, shape, cuts, least, high):
    factor_of, own = 1.0, jax.random.fold_in(stream_key, 6)
    for position, shards_of in cuts:
        draws = jnp.exp(jax.random.uniform(jax.random.fold_in(own, position), (shards_of,), jnp.float32, least / len(cuts), high / len(cuts)))
        factor_of = factor_of * jnp.repeat(draws, shape[position] // shards_of).reshape([-1 if axis == position else 1 for axis in range(len(shape))])
    return factor_of


def assign_block(key, own, number, rows, number_of, top, most, slope):
    order = jax.random.permutation(key, number_of)
    crowded, usual = portions_of(number_of, rows * top, most, slope, True), portions_of(number_of, rows * top, most, slope, False)
    places = jnp.arange(number_of)

    def named(sizes, rotation):
        used = int((sizes > 0).sum())
        fixed = max(1, used // 4)
        shifted = fixed + (places - fixed + rotation * (used - fixed)) % max(1, number_of - fixed)
        return jnp.zeros((number_of,), jnp.int32).at[order[jnp.where(places < fixed, places, shifted)]].set(jnp.asarray(sizes, jnp.int32))

    sizes = jnp.where(number % 4 == 0, named(crowded, number // 4), named(usual, number - number // 4 - 1))
    mixed = jax.random.permutation(jax.random.fold_in(own, 3), number_of)
    source_of, sink = mixed[0:number_of // 2 * 2:2], mixed[1:number_of // 2 * 2:2]
    room = jnp.minimum(sizes[source_of] - 1, most - sizes[sink]) // 2
    room = jnp.where((source_of == order[0]) | (sink == order[0]) | (sizes[sink] == 0), 0, jnp.maximum(room, 0))
    shifted = jax.random.randint(jax.random.fold_in(own, 4), (number_of // 2,), 0, 1 << 20) % (room + 1)
    sizes = sizes.at[source_of].add(-shifted).at[sink].add(shifted)
    items = jnp.searchsorted(jnp.cumsum(sizes), jnp.arange(rows * top), side="right").astype(jnp.int32)
    grid = items.reshape(top, rows).T
    grid = grid[jax.random.permutation(jax.random.fold_in(own, 1), rows)]
    rotation = jax.random.randint(jax.random.fold_in(own, 2), (rows, 1), 0, top)
    return jnp.take_along_axis(grid, (jnp.arange(top)[None, :] + rotation) % top, axis=1)


def portions_of(number_of, total, most, skew, full):
    weights = [(1 << 20) // math.isqrt(rank ** skew) + 1 for rank in range(1, number_of + 1)]
    largest = most if full else min(most, max(-(-total // number_of), total * weights[0] // sum(weights)))
    least = 1 if total - largest >= number_of - 1 else 0
    holding, rest = [largest] + [least] * (number_of - 1), total - largest - least * (number_of - 1)
    while rest > 0:
        free = [i for i in range(1, number_of) if holding[i] < largest] or [i for i in range(1, number_of) if holding[i] < most]
        pool, remaining = sum([weights[i] for i in free]), rest
        for i in free:
            addition = min(most - holding[i], max(1, remaining * weights[i] // pool), rest)
            holding[i] = holding[i] + addition
            rest = rest - addition
    return np.array(holding)


def centred(rng, extent, scale, bound, cuts=(), kind=jnp.bfloat16):
    drawn = scale * jax.random.normal(rng, extent, jnp.float32)
    if cuts:
        drawn = drawn * steps_of(rng, extent, cuts, -0.22, 0.18)
    return jnp.clip(drawn, -bound, bound).astype(kind)


def setup_inputs(seed: int = 0) -> dict:
    splits = jax.random.split(jax.random.key(seed), 12)
    hidden = draw_hidden(jax.random.fold_in(splits[11], 71), 0)
    norm_gain = jnp.clip(1.0 + 0.18 * jax.random.normal(splits[1], (D,), jnp.float32), 0.099609375, 1.8984375).astype(jnp.bfloat16)
    q_weight = centred(splits[2], (D, HEADS * HD), D ** -0.5, 0.0625, ((0, 128),))
    k_weight = centred(splits[3], (D, KV * HD), D ** -0.5, 0.0625, ((0, 128),))
    v_weight = centred(splits[4], (D, KV * HD), D ** -0.5, 0.0625, ((0, 128),))
    o_weight = centred(splits[5], (D, HEADS * HD), (HEADS * HD) ** -0.5, 0.0625, ((0, 128),))
    key_cache = draw_key_cache(jax.random.fold_in(splits[11], 71), 0)
    value_cache = draw_value_cache(jax.random.fold_in(splits[11], 71), 0)
    cache_len = draw_cache_len(jax.random.fold_in(splits[11], 71), 0)
    finish = set_ends(jax.random.randint(splits[9], (ROWS,), 0, STEPS + 1), jax.random.fold_in(splits[9], 1), 0, STEPS).astype(jnp.int32)
    owner_keys = jax.random.split(jax.random.fold_in(splits[10], 1), ROWS // ROWS_REP)
    owner_turns = jax.random.permutation(jax.random.fold_in(splits[10], 3), ROWS // ROWS_REP)
    owner = jax.vmap(lambda own, number: assign_block(jax.random.fold_in(splits[10], 2), own, number, ROWS_REP, N_REP * N_TP, 1, CAP, 2))(owner_keys, owner_turns).reshape((ROWS, 1))
    return dict(hidden=hidden, norm_gain=norm_gain, q_weight=q_weight, k_weight=k_weight, v_weight=v_weight, o_weight=o_weight, key_cache=key_cache, value_cache=value_cache, cache_len=cache_len, finish=finish, owner=owner)


def rotate_half(values, angles):
    half = values.shape[-1] // 2
    first = values[..., :half]
    second = values[..., half:]
    cosine = jnp.cos(angles)
    sine = jnp.sin(angles)
    return jnp.concatenate([first * cosine - second * sine, second * cosine + first * sine], axis=-1)

def rope_angles(positions, head_size):
    half = head_size // 2
    freqs = 500000.0 ** (-(jnp.arange(half, dtype=jnp.float32) * 2.0) / head_size)
    return positions.astype(jnp.float32)[..., None] * freqs

def attend_block(block):
    query, key_new, value_new, key_old, value_old, lengths = block
    group_count = query.shape[3]
    scale = 1.0 / jnp.sqrt(jnp.float32(HD))
    query_f = query.astype(jnp.float32)
    old_scores = jnp.einsum('srkgd,rkjd->srkgj', query_f, key_old.astype(jnp.float32)) * scale
    new_scores = jnp.einsum('srkgd,trkd->srkgt', query_f, key_new.astype(jnp.float32)) * scale
    old_mask = jnp.arange(CACHE)[None, None, None, None, :] < lengths[None, :, None, None, None]
    step_ids = jnp.arange(STEPS)
    new_mask = step_ids[None, :] <= step_ids[:, None]
    new_mask = new_mask[:, None, None, None, :]
    old_scores = jnp.where(old_mask, old_scores, -jnp.inf)
    new_scores = jnp.where(new_mask, new_scores, -jnp.inf)
    top = jnp.maximum(lax.optimization_barrier(jnp.max(old_scores, -1, keepdims=True)), lax.optimization_barrier(jnp.max(new_scores, -1, keepdims=True)))
    old_exp = jnp.exp(old_scores - top)
    new_exp = jnp.exp(new_scores - top)
    total = lax.optimization_barrier(jnp.sum(old_exp, -1, keepdims=True)) + lax.optimization_barrier(jnp.sum(new_exp, -1, keepdims=True))
    old_probs = (old_exp / total).astype(jnp.bfloat16).astype(jnp.float32)
    new_probs = (new_exp / total).astype(jnp.bfloat16).astype(jnp.float32)
    output = jnp.einsum('srkgj,rkjd->srkgd', old_probs, value_old.astype(jnp.float32))
    output = output + jnp.einsum('srkgt,trkd->srkgd', new_probs, value_new.astype(jnp.float32))
    return output.astype(jnp.bfloat16)

def reference(hidden, norm_gain, q_weight, k_weight, v_weight, o_weight, key_cache, value_cache, cache_len, finish, owner):
    group_size = HEADS // KV
    hidden_f = hidden.astype(jnp.float32)
    mean_square = lax.optimization_barrier(jnp.mean(hidden_f * hidden_f, axis=-1, keepdims=True))
    normed = (hidden_f * lax.rsqrt(mean_square + 1e-05) * norm_gain.astype(jnp.float32)).astype(jnp.bfloat16)
    flat = normed.reshape(STEPS * ROWS, D)
    query = jnp.dot(flat, q_weight, preferred_element_type=jnp.float32).reshape(STEPS, ROWS, HEADS, HD)
    key_new = jnp.dot(flat, k_weight, preferred_element_type=jnp.float32).reshape(STEPS, ROWS, KV, HD)
    value_new = jnp.dot(flat, v_weight, preferred_element_type=jnp.float32).reshape(STEPS, ROWS, KV, HD)
    positions = cache_len[None, :] + jnp.arange(STEPS, dtype=jnp.int32)[:, None]
    angles = rope_angles(positions, HD)[:, :, None, :]
    query = rotate_half(query, angles).astype(jnp.bfloat16)
    key_new = rotate_half(key_new, angles).astype(jnp.bfloat16)
    value_new = value_new.astype(jnp.bfloat16)
    key_old = key_cache[:, ::DUP]
    value_old = value_cache[:, ::DUP]
    query_b = query.reshape(STEPS, N_REP, ROWS_REP, KV, group_size, HD).transpose(1, 0, 2, 3, 4, 5)
    key_b = key_new.reshape(STEPS, N_REP, ROWS_REP, KV, HD).transpose(1, 0, 2, 3, 4)
    value_b = value_new.reshape(STEPS, N_REP, ROWS_REP, KV, HD).transpose(1, 0, 2, 3, 4)
    key_old_b = key_old.reshape(N_REP, ROWS_REP, KV, CACHE, HD)
    value_old_b = value_old.reshape(N_REP, ROWS_REP, KV, CACHE, HD)
    length_b = cache_len.reshape(N_REP, ROWS_REP)
    attn = lax.map(attend_block, (query_b, key_b, value_b, key_old_b, value_old_b, length_b))
    attn = attn.transpose(1, 0, 2, 3, 4, 5).reshape(STEPS * ROWS, HEADS * HD)
    projected = jnp.dot(attn, o_weight.T, preferred_element_type=jnp.float32).reshape(STEPS, ROWS, D)
    active = jnp.arange(STEPS, dtype=jnp.int32)[:, None] <= finish[None, :]
    decoded = jnp.where(active[:, :, None], hidden_f + projected, 0.0).astype(jnp.bfloat16)
    chosen = jnp.arange(STEPS, dtype=jnp.int32)[:, None] == finish[None, :]
    at_finish = lax.optimization_barrier(jnp.sum(jnp.where(chosen[:, :, None], decoded.astype(jnp.float32), 0.0), axis=0))
    is_returned = finish < STEPS
    owner_flat = owner[:, 0]
    owner_b = owner_flat.reshape(N_REP, ROWS_REP)
    returned_b = is_returned.reshape(N_REP, ROWS_REP)
    row_ids = jnp.arange(ROWS_REP)
    earlier = row_ids[None, :] < row_ids[:, None]
    same = (owner_b[:, :, None] == owner_b[:, None, :]) & returned_b[:, None, :] & earlier[None, :, :]
    rank = lax.optimization_barrier(jnp.sum(same.astype(jnp.int32), axis=-1)).reshape(ROWS)
    replica = (jnp.arange(ROWS, dtype=jnp.int32) // ROWS_REP).astype(jnp.int32)
    slot_total = N_REP * N_TP * N_REP * CAP
    slot = jnp.where(is_returned, owner_flat * (N_REP * CAP) + rank * N_REP + replica, slot_total).astype(jnp.int32)
    buffer = jnp.zeros((slot_total + 1, D), jnp.float32).at[slot].set(at_finish)
    returned = buffer[:slot_total].astype(jnp.bfloat16)
    return (decoded, returned)
```

```python
import jax
import jax.numpy as jnp
from jax import lax
from jax.sharding import PartitionSpec as P

KV = 8


def rotate_half(values, angles):
    half = values.shape[-1] // 2
    first = values[..., :half]
    second = values[..., half:]
    cosine = jnp.cos(angles)
    sine = jnp.sin(angles)
    return jnp.concatenate(
        [first * cosine - second * sine, second * cosine + first * sine], axis=-1
    )


def per_device(
    hidden,
    norm_gain,
    q_weight,
    k_weight,
    v_weight,
    o_weight,
    key_cache,
    value_cache,
    cache_len,
    finish,
    owner,
):
    tp_count = lax.axis_size("tp")
    rep_count = lax.axis_size("rep")
    tp_index = lax.axis_index("tp")
    step_count, row_count, model_width = hidden.shape
    head_size = key_cache.shape[-1]
    cache_size = key_cache.shape[2]
    local_rows = q_weight.shape[0]
    share = model_width // tp_count
    pair_weight = jnp.concatenate(
        [
            k_weight.reshape(local_rows, KV, 1, head_size),
            v_weight.reshape(local_rows, KV, 1, head_size),
        ],
        axis=2,
    )
    kv_spread = jnp.repeat(pair_weight, tp_count // KV, axis=1).reshape(
        local_rows, tp_count * 2 * head_size
    )
    query_part, kv_part = (
        lax.all_to_all(q_weight, "tp", split_axis=1, concat_axis=0, tiled=True),
        lax.all_to_all(kv_spread, "tp", split_axis=1, concat_axis=0, tiled=True),
    )
    hidden_f = hidden.astype(jnp.float32)
    mean_square = jnp.mean(hidden_f * hidden_f, axis=-1, keepdims=True)
    normed = (hidden_f * lax.rsqrt(mean_square + 1e-05) * norm_gain.astype(jnp.float32)).astype(
        jnp.bfloat16
    )
    token_count = step_count * row_count
    normed_flat = normed.reshape(token_count, model_width)
    query_full, kv_full = (
        lax.all_gather(query_part, "rep", axis=0, tiled=True),
        lax.all_gather(kv_part, "rep", axis=0, tiled=True),
    )
    query_proj = jnp.dot(normed_flat, query_full, preferred_element_type=jnp.float32)
    kv_proj = jnp.dot(normed_flat, kv_full, preferred_element_type=jnp.float32)
    heads_here = query_proj.shape[1] // head_size
    positions = cache_len[None, :] + jnp.arange(step_count, dtype=jnp.int32)[:, None]
    half = head_size // 2
    freqs = 500000.0 ** (-(jnp.arange(half, dtype=jnp.float32) * 2.0) / head_size)
    angles = (positions.astype(jnp.float32)[..., None] * freqs).reshape(token_count, 1, half)
    query_rot = rotate_half(query_proj.reshape(token_count, heads_here, head_size), angles).astype(
        jnp.bfloat16
    )
    key_rot = rotate_half(kv_proj[:, :head_size], angles[:, 0, :]).astype(jnp.bfloat16)
    value_new = kv_proj[:, head_size:].astype(jnp.bfloat16)
    query_rows = query_rot.reshape(step_count, row_count, heads_here, head_size).transpose(
        1, 0, 2, 3
    )
    query_rows = query_rows.reshape(row_count, step_count * heads_here, head_size)
    key_rows = key_rot.reshape(step_count, row_count, head_size).transpose(1, 0, 2)
    value_rows = value_new.reshape(step_count, row_count, head_size).transpose(1, 0, 2)
    key_old = key_cache[:, 0]
    value_old = value_cache[:, 0]
    scale = 1.0 / jnp.sqrt(jnp.float32(head_size))
    old_scores = (
        jnp.einsum("rqd,rjd->rqj", query_rows, key_old, preferred_element_type=jnp.float32) * scale
    )
    new_scores = (
        jnp.einsum("rqd,rtd->rqt", query_rows, key_rows, preferred_element_type=jnp.float32) * scale
    )
    old_mask = jnp.arange(cache_size)[None, None, :] < cache_len[:, None, None]
    query_step = jnp.arange(step_count * heads_here) // heads_here
    new_mask = (jnp.arange(step_count)[None, :] <= query_step[:, None])[None, :, :]
    old_scores = jnp.where(old_mask, old_scores, -jnp.inf)
    new_scores = jnp.where(new_mask, new_scores, -jnp.inf)
    top = jnp.maximum(
        jnp.max(old_scores, -1, keepdims=True), jnp.max(new_scores, -1, keepdims=True)
    )
    old_exp = jnp.exp(old_scores - top)
    new_exp = jnp.exp(new_scores - top)
    total = jnp.sum(old_exp, -1, keepdims=True) + jnp.sum(new_exp, -1, keepdims=True)
    old_probs = (old_exp / total).astype(jnp.bfloat16)
    new_probs = (new_exp / total).astype(jnp.bfloat16)
    attended = jnp.einsum("rqj,rjd->rqd", old_probs, value_old, preferred_element_type=jnp.float32)
    attended = attended + jnp.einsum(
        "rqt,rtd->rqd", new_probs, value_rows, preferred_element_type=jnp.float32
    )
    attended = attended.astype(jnp.bfloat16).reshape(row_count, step_count, heads_here, head_size)
    attended = attended.transpose(1, 0, 2, 3).reshape(token_count, heads_here * head_size)
    attended_full = lax.all_gather(attended, "tp", axis=1, tiled=True)
    out_rows = lax.all_gather(o_weight, "rep", axis=0, tiled=True)
    head_total = lax.dot_general(
        attended_full, out_rows, (((1,), (1,)), ((), ())), preferred_element_type=jnp.float32
    ).reshape(step_count, row_count, share)
    residual = lax.dynamic_slice_in_dim(hidden_f, tp_index * share, share, 2)
    active = jnp.arange(step_count, dtype=jnp.int32)[:, None] <= finish[None, :]
    decoded = jnp.where(active[:, :, None], head_total + residual, 0.0).astype(jnp.bfloat16)
    chosen = jnp.arange(step_count, dtype=jnp.int32)[:, None] == finish[None, :]
    at_finish = jnp.sum(jnp.where(chosen[:, :, None], decoded.astype(jnp.float32), 0.0), axis=0)
    is_returned = finish < step_count
    owner_flat = owner[:, 0]
    row_ids = jnp.arange(row_count)
    same = (
        (owner_flat[:, None] == owner_flat[None, :])
        & is_returned[None, :]
        & (row_ids[None, :] < row_ids[:, None])
    )
    rank = jnp.sum(same.astype(jnp.int32), axis=1)
    device_count = rep_count * tp_count
    capacity = max(2, 2 * row_count // device_count)
    slot = jnp.where(is_returned, owner_flat * capacity + rank, -1)
    one_hot = (jnp.arange(device_count * capacity)[:, None] == slot[None, :]).astype(jnp.bfloat16)
    outgoing = jnp.dot(
        one_hot, at_finish.astype(jnp.bfloat16), preferred_element_type=jnp.float32
    ).astype(jnp.bfloat16)
    arrived = lax.all_to_all(
        outgoing.reshape(device_count, capacity, share),
        ("rep", "tp"),
        split_axis=0,
        concat_axis=2,
        tiled=True,
    )
    returned = arrived.reshape(capacity * rep_count, model_width)
    return (decoded, returned)


def solution(mesh):
    placed = (
        P(None, "rep", None),
        P(),
        P(("rep", "tp"), None),
        P(("rep", "tp"), None),
        P(("rep", "tp"), None),
        P(("tp", "rep"), None),
        P("rep", "tp", None, None),
        P("rep", "tp", None, None),
        P("rep"),
        P("rep"),
        P("rep", None),
    )
    return jax.shard_map(
        per_device,
        mesh=mesh,
        in_specs=placed,
        out_specs=(P(None, "rep", "tp"), P(("rep", "tp"), None)),
        check_vma=False,
    )
```

```python
import jax
import jax.numpy as jnp
from jax import lax
from jax.experimental import pallas as pl
from jax.experimental.pallas import tpu as pltpu
from jax.sharding import PartitionSpec as P

MESH = pl.DeviceIdType.MESH
KV = 8
STEPS = 4
ROWS = 128
HD = 128
CACHE = 192
KEYS = CACHE + 16
D = 8192
REP = 8
TP = 16
QC = 512
WC = QC + HD
SHARD = 64
BLOCK = TP * SHARD
TOKENS = STEPS * ROWS
CHUNKS = 4
CROWS = ROWS // CHUNKS
CTOK = CROWS * STEPS
EPS = 1e-05

QKV_CUT = 576
OUT_CUT = 5120


def kernel(
    hidden,
    gain,
    q_weight,
    k_weight,
    v_weight,
    o_weight,
    key_cache,
    value_cache,
    lens,
    finish,
    cosine,
    sine,
    one_hot,
    decoded,
    returned,
    staged,
    normed,
    weights,
    out_rows,
    keys,
    values,
    acc,
    queries,
    pair,
    attn_rows,
    gathered,
    out_acc,
    residual,
    at_finish,
    outgoing,
    stage_one,
    spread,
    stage_two,
    arrived,
    load_sem,
    local_sem,
    a2a_send,
    a2a_recv,
    qkv_send,
    qkv_recv,
    out_send,
    out_recv,
    pair_send,
    pair_recv,
    attn_send,
    attn_recv,
    one_send,
    one_recv,
    two_send,
    two_recv,
):
    rep = lax.axis_index("rep")
    tp = lax.axis_index("tp")
    y, x = rep // 4, rep % 4
    across = (1 - y) * 4
    mine = y * 4
    east, west, far = (x + 1) % 4, (x + 3) % 4, (x + 2) % 4
    rep_east, rep_west, rep_y = mine + east, mine + west, across + x
    z, low = tp // 4, tp % 4
    core_peer = tp + 1 - 2 * (tp % 2)
    hi_peer = tp + 2 - 4 * ((tp // 2) % 2)
    pending = []

    def send(src, dst, sends, recvs, k, to):
        copy = pltpu.make_async_remote_copy(
            src_ref=src,
            dst_ref=dst,
            send_sem=sends.at[k],
            recv_sem=recvs.at[k],
            device_id=to,
            device_id_type=MESH,
        )
        copy.start()
        pending.append(copy)

    def receive(region, sends, recvs, k):
        pltpu.make_async_remote_copy(
            src_ref=region,
            dst_ref=region,
            send_sem=sends.at[k],
            recv_sem=recvs.at[k],
            device_id=(rep, core_peer),
            device_id_type=MESH,
        ).wait_recv()

    barrier = pltpu.get_barrier_semaphore()
    for d in range(1, TP):
        pl.semaphore_signal(
            barrier, inc=1, device_id=(rep, (tp + d) % TP), device_id_type=MESH
        )
    for d in range(1, REP):
        pl.semaphore_signal(
            barrier, inc=1, device_id=((rep + d) % REP, tp), device_id_type=MESH
        )
    key_load = pltpu.make_async_copy(
        key_cache.at[:, 0], keys.at[:, pl.ds(0, CACHE), :], local_sem.at[0]
    )
    value_load = pltpu.make_async_copy(
        value_cache.at[:, 0], values.at[:, pl.ds(0, CACHE), :], local_sem.at[1]
    )
    my_cols = pl.ds(pl.multiple_of(tp * QC, QC), QC)
    residual_load = pltpu.make_async_copy(
        hidden.at[:, :, my_cols], residual, local_sem.at[2]
    )
    my_rows = pl.ds(pl.multiple_of(tp * SHARD, SHARD), SHARD)
    q_load = pltpu.make_async_copy(
        q_weight.at[:, my_cols], weights.at[rep, my_rows, pl.ds(0, QC)], local_sem.at[3]
    )
    kv_cols = pl.ds(pl.multiple_of((tp // 2) * HD, HD), HD)
    my_kv = weights.at[rep, my_rows, pl.ds(QC, HD)]
    k_load = pltpu.make_async_copy(k_weight.at[:, kv_cols], my_kv, local_sem.at[4])
    v_load = pltpu.make_async_copy(v_weight.at[:, kv_cols], my_kv, local_sem.at[4])

    def out_block(r, part):
        start, size = {
            "A": (0, OUT_CUT),
            "A0": (0, OUT_CUT // 2),
            "A1": (OUT_CUT // 2, OUT_CUT // 2),
            "B": (OUT_CUT, D - OUT_CUT),
            "B0": (OUT_CUT, (D - OUT_CUT) // 2),
            "B1": (OUT_CUT + (D - OUT_CUT) // 2, (D - OUT_CUT) // 2),
            "all": (0, D),
        }[part]
        return out_rows.at[
            pl.ds(pl.multiple_of(r * SHARD, SHARD), SHARD), pl.ds(start, size)
        ]

    def qkv_block(r, part):
        start, size = {
            "A": (0, QKV_CUT),
            "A0": (0, QKV_CUT // 2),
            "A1": (QKV_CUT // 2, QKV_CUT // 2),
            "B": (QKV_CUT, BLOCK - QKV_CUT),
            "B0": (QKV_CUT, (BLOCK - QKV_CUT) // 2),
            "B1": (QKV_CUT + (BLOCK - QKV_CUT) // 2, (BLOCK - QKV_CUT) // 2),
        }[part]
        return weights.at[r, pl.ds(start, size), :]

    out_load = pltpu.make_async_copy(o_weight, out_block(rep, "all"), local_sem.at[5])
    q_load.start()
    pl.when(tp % 2 == 0)(k_load.start)
    pl.when(tp % 2 == 1)(v_load.start)
    out_load.start()

    def hidden_load(step, slot):
        return pltpu.make_async_copy(
            hidden.at[step // CHUNKS, pl.ds(pl.multiple_of((step % CHUNKS) * CROWS, CROWS), CROWS), :],
            staged.at[slot],
            load_sem.at[slot],
        )

    hidden_load(0, 0).start()
    pl.semaphore_wait(barrier, TP - 1 + REP - 1)

    for d in range(1, TP):
        to = (tp + d) % TP
        there = (rep, to)
        send(
            q_weight.at[:, pl.ds(pl.multiple_of(to * QC, QC), QC)],
            weights.at[rep, my_rows, pl.ds(0, QC)],
            a2a_send,
            a2a_recv,
            d,
            there,
        )
        cols = pl.ds(pl.multiple_of((to // 2) * HD, HD), HD)

        def kv_copy(source, cols=cols, d=d, there=there):
            return pltpu.make_async_remote_copy(
                src_ref=source.at[:, cols],
                dst_ref=weights.at[rep, my_rows, pl.ds(QC, HD)],
                send_sem=a2a_send.at[TP + d],
                recv_sem=a2a_recv.at[TP + d],
                device_id=there,
                device_id_type=MESH,
            )

        from_k, from_v = kv_copy(k_weight), kv_copy(v_weight)
        pl.when(to % 2 == 0)(from_k.start)
        pl.when(to % 2 == 1)(from_v.start)
        pending.append(from_k)

    east_dev, west_dev, y_dev = (rep_east, tp), (rep_west, tp), (rep_y, tp)

    def ring(block, sends, recvs):
        def go(k, r, part, to, src=None):
            send(src if src is not None else block(r, part), block(r, part), sends, recvs, k, to)

        def got(k, r, part):
            receive(block(r, part), sends, recvs, k)

        return go, got

    o_go, o_got = ring(out_block, out_send, out_recv)
    w_go, w_got = ring(qkv_block, qkv_send, qkv_recv)

    o_a = o_weight.at[:, pl.ds(0, OUT_CUT)]
    o_b = o_weight.at[:, pl.ds(OUT_CUT, D - OUT_CUT)]
    o_go(9, rep, "B", east_dev, o_b)
    o_go(10, rep, "B", west_dev, o_b)
    o_go(0, rep, "A", y_dev, o_a)
    o_go(1, rep, "A", east_dev, o_a)
    o_go(2, rep, "A", west_dev, o_a)

    key_load.start()
    value_load.start()
    residual_load.start()

    def norm_step(step, carry):
        slot = step % 2
        hidden_load(step, slot).wait()

        @pl.when(step + 1 < STEPS * CHUNKS)
        def _():
            hidden_load(step + 1, 1 - slot).start()

        values_f = staged[slot].astype(jnp.float32)
        mean = jnp.mean(values_f * values_f, axis=-1, keepdims=True)
        scale = lax.rsqrt(mean + EPS)
        out = (values_f * scale * gain[...].astype(jnp.float32)).astype(jnp.bfloat16)
        rows = pl.ds(pl.multiple_of(step * CROWS, CROWS), CROWS)
        for r in range(REP):
            normed[r, rows, :] = out[:, r * BLOCK : (r + 1) * BLOCK]
        return carry

    lax.fori_loop(0, STEPS * CHUNKS, norm_step, 0)

    q_load.wait()
    k_load.wait()
    for d in range(1, TP):
        source = (tp + TP - d) % TP
        rows = pl.ds(pl.multiple_of(source * SHARD, SHARD), SHARD)
        receive(weights.at[rep, rows, pl.ds(0, QC)], a2a_send, a2a_recv, d)
        receive(weights.at[rep, rows, pl.ds(QC, HD)], a2a_send, a2a_recv, TP + d)

    def project(r, first=False):
        def tile(m, carry):
            rows = pl.ds(pl.multiple_of(m * 256, 256), 256)
            part = jnp.dot(normed[r, rows, :], weights[r], preferred_element_type=jnp.float32)
            if first:
                acc[rows, :] = part
            else:
                acc[rows, :] += part
            return carry

        lax.fori_loop(0, TOKENS // 256, tile, 0)

    w_go(9, rep, "B", east_dev)
    w_go(10, rep, "B", west_dev)
    w_go(0, rep, "A", y_dev)
    w_go(1, rep, "A", east_dev)
    w_go(2, rep, "A", west_dev)
    w_go(11, rep, "B", y_dev)
    project(rep, True)
    w_got(9, mine + west, "B")
    w_go(12, mine + west, "B0", east_dev)
    w_go(14, mine + west, "B", y_dev)
    w_got(10, mine + east, "B")
    w_go(13, mine + east, "B1", west_dev)
    w_go(15, mine + east, "B", y_dev)
    w_got(0, rep_y, "A")
    w_go(3, rep_y, "A", east_dev)
    w_go(4, rep_y, "A", west_dev)
    w_got(1, mine + west, "A")
    w_go(5, mine + west, "A0", east_dev)
    w_got(2, mine + east, "A")
    w_go(6, mine + east, "A1", west_dev)
    project(mine + west)
    project(mine + east)
    w_got(12, mine + far, "B0")
    w_go(16, mine + far, "B0", y_dev)
    w_got(13, mine + far, "B1")
    w_go(17, mine + far, "B1", y_dev)
    w_got(11, rep_y, "B")
    project(rep_y)
    w_got(3, across + west, "A")
    w_go(7, across + west, "A0", east_dev)
    w_got(4, across + east, "A")
    w_go(8, across + east, "A1", west_dev)

    o_go(11, rep, "B", y_dev, o_b)
    o_got(9, mine + west, "B")
    o_got(10, mine + east, "B")
    o_got(0, rep_y, "A")
    o_got(1, mine + west, "A")
    o_got(2, mine + east, "A")
    o_go(12, mine + west, "B0", east_dev)
    o_go(13, mine + east, "B1", west_dev)
    o_go(14, mine + west, "B", y_dev)
    o_go(15, mine + east, "B", y_dev)
    o_go(3, rep_y, "A", east_dev)
    o_go(4, rep_y, "A", west_dev)
    o_go(5, mine + west, "A0", east_dev)
    o_go(6, mine + east, "A1", west_dev)

    w_got(14, across + west, "B")
    project(across + west)
    w_got(15, across + east, "B")
    project(across + east)
    w_got(5, mine + far, "A0")
    w_got(6, mine + far, "A1")
    project(mine + far)
    w_got(7, across + far, "A0")
    w_got(8, across + far, "A1")
    w_got(16, across + far, "B0")
    w_got(17, across + far, "B1")
    project(across + far)

    def rotate(block, rows):
        return block * cosine[rows, :] + pltpu.roll(block, HD // 2, 1) * sine[rows, :]

    is_key = tp % 2 == 0
    for step in range(STEPS):
        rows = pl.ds(step * ROWS, ROWS)
        block = acc[rows, QC:WC]
        pair[0, rows, :] = jnp.where(is_key, rotate(block, rows), block).astype(jnp.bfloat16)
    send(pair.at[0], pair.at[1], pair_send, pair_recv, 0, (rep, core_peer))
    for step in range(STEPS):
        rows = pl.ds(step * ROWS, ROWS)
        for h in range(QC // HD):
            queries[:, step * 4 + h, :] = rotate(acc[rows, h * HD : (h + 1) * HD], rows)
    receive(pair.at[1], pair_send, pair_recv, 0)
    key_load.wait()
    value_load.wait()
    zeros = jnp.zeros((ROWS, 16, HD), jnp.float32)
    for place, target in ((0, keys), (1, values)):
        spread[...] = zeros
        slot = (tp + place) % 2
        for step in range(STEPS):
            spread[:, step, :] = pair[slot, pl.ds(step * ROWS, ROWS), :].astype(jnp.float32)
        target[:, pl.ds(CACHE, 16), :] = spread[...].astype(jnp.bfloat16)

    column = lax.broadcasted_iota(jnp.int32, (16, KEYS), 1)
    step_of = lax.broadcasted_iota(jnp.int32, (16, KEYS), 0) // 4
    new_ok = (column >= CACHE) & (column - CACHE <= step_of)
    score_scale = 1.0 / (float(HD) ** 0.5)

    def attend(chunk):
        def rows_of_8(it, carry):
            for u in range(8):
                local = it * 8 + u
                i = chunk * CROWS + local
                query = queries[i].astype(jnp.bfloat16)
                scores = lax.dot_general(
                    query, keys[i], (((1,), (1,)), ((), ())), preferred_element_type=jnp.float32
                )
                valid = (column < jnp.minimum(lens[i], CACHE)) | new_ok
                scores = jnp.where(valid, scores * score_scale, -1e30)
                top = jnp.max(scores, axis=-1, keepdims=True)
                weight = jnp.exp(scores - top)
                total = jnp.sum(weight, axis=-1, keepdims=True)
                probs = (weight / total).astype(jnp.bfloat16)
                attn_rows[local] = jnp.dot(probs, values[i], preferred_element_type=jnp.float32)
            return carry

        lax.fori_loop(0, CROWS // 8, rows_of_8, 0)
        for step in range(STEPS):
            for h in range(QC // HD):
                gathered[
                    tp,
                    pl.ds(chunk * CTOK + step * CROWS, CROWS),
                    pl.ds(h * HD, HD),
                ] = attn_rows[:, step * 4 + h, :].astype(jnp.bfloat16)

    def attn_block(t, chunk, part="all"):
        start, size = {"all": (0, CTOK), "0": (0, CTOK // 2), "1": (CTOK // 2, CTOK // 2)}[part]
        return gathered.at[t, pl.ds(chunk * CTOK + start, size), :]

    z_up, z_down, z_far = (z + 1) % 4 * 4, (z + 3) % 4 * 4, (z + 2) % 4 * 4
    low_hi = hi_peer % 4
    up_dev, down_dev = (rep, z_up + low), (rep, z_down + low)
    hi_dev, core_dev = (rep, hi_peer), (rep, core_peer)
    PER = 18

    def a_go(chunk, k, t, to, part="all"):
        block = attn_block(t, chunk, part)
        send(block, block, attn_send, attn_recv, chunk * PER + k, to)

    def a_got(chunk, k, t, part="all"):
        receive(attn_block(t, chunk, part), attn_send, attn_recv, chunk * PER + k)

    def gather_first(chunk):
        a_go(chunk, 0, tp, hi_dev)
        a_go(chunk, 1, tp, up_dev)
        a_go(chunk, 2, tp, down_dev)
        a_go(chunk, 3, tp, core_dev)

    def gather_second(chunk):
        a_got(chunk, 0, hi_peer)
        a_go(chunk, 4, hi_peer, up_dev)
        a_go(chunk, 5, hi_peer, down_dev)
        a_got(chunk, 1, z_down + low)
        a_go(chunk, 7, z_down + low, up_dev, "0")
        a_got(chunk, 2, z_up + low)
        a_go(chunk, 8, z_up + low, down_dev, "1")
        a_go(chunk, 6, hi_peer, core_dev)
        a_go(chunk, 9, z_down + low, core_dev)
        a_go(chunk, 10, z_up + low, core_dev)

    def gather_third(chunk):
        a_got(chunk, 4, z_down + low_hi)
        a_go(chunk, 11, z_down + low_hi, up_dev, "0")
        a_got(chunk, 5, z_up + low_hi)
        a_go(chunk, 12, z_up + low_hi, down_dev, "1")
        a_go(chunk, 13, z_down + low_hi, core_dev)
        a_go(chunk, 14, z_up + low_hi, core_dev)
        a_got(chunk, 7, z_far + low, "0")
        a_got(chunk, 8, z_far + low, "1")
        a_go(chunk, 15, z_far + low, core_dev)

    def gather_fourth(chunk):
        a_got(chunk, 11, z_far + low_hi, "0")
        a_got(chunk, 12, z_far + low_hi, "1")
        a_go(chunk, 16, z_far + low_hi, core_dev)

    low_core = core_peer % 4
    low_both = (low_hi + 1) - 2 * (low_hi % 2)

    def gather_last(chunk):
        a_got(chunk, 3, core_peer)
        a_got(chunk, 6, z * 4 + low_both)
        a_got(chunk, 9, z_down + low_core)
        a_got(chunk, 10, z_up + low_core)
        a_got(chunk, 13, z_down + low_both)
        a_got(chunk, 14, z_up + low_both)
        a_got(chunk, 15, z_far + low_core)
        a_got(chunk, 16, z_far + low_both)

    attend(0)
    gather_first(0)
    o_got(12, mine + far, "B0")
    o_go(16, mine + far, "B0", y_dev)
    o_got(13, mine + far, "B1")
    o_go(17, mine + far, "B1", y_dev)
    attend(1)
    gather_first(1)
    gather_second(0)
    attend(2)
    gather_first(2)
    gather_second(1)
    gather_third(0)
    o_got(3, across + west, "A")
    o_go(7, across + west, "A0", east_dev)
    o_got(4, across + east, "A")
    o_go(8, across + east, "A1", west_dev)
    attend(3)
    gather_first(3)
    gather_second(2)
    gather_third(1)
    gather_fourth(0)
    gather_second(3)
    gather_third(2)
    gather_fourth(1)
    gather_third(3)
    gather_fourth(2)
    gather_fourth(3)

    out_load.wait()
    o_got(5, mine + far, "A0")
    o_got(6, mine + far, "A1")
    o_got(11, rep_y, "B")
    o_got(14, across + west, "B")
    o_got(15, across + east, "B")
    o_got(7, across + far, "A0")
    o_got(8, across + far, "A1")
    o_got(16, across + far, "B0")
    o_got(17, across + far, "B1")
    for chunk in range(CHUNKS):
        gather_last(chunk)

    out_acc[...] = jnp.zeros_like(out_acc)

    def out_step(t, carry):
        cols = pl.ds(pl.multiple_of(t * QC, QC), QC)
        out_acc[...] += lax.dot_general(
            gathered[t], out_rows[:, cols], (((1,), (1,)), ((), ())), preferred_element_type=jnp.float32
        )
        return carry

    lax.fori_loop(0, TP, out_step, 0)

    residual_load.wait()
    for chunk in range(CHUNKS):
        rows = pl.ds(chunk * CROWS, CROWS)
        ends = finish[rows, :]
        picked = jnp.zeros((CROWS, QC), jnp.float32)
        for step in range(STEPS):
            total = out_acc[pl.ds(chunk * CTOK + step * CROWS, CROWS), :]
            total = total + residual[step, rows, :].astype(jnp.float32)
            kept = jnp.where(ends >= step, total, 0.0).astype(jnp.bfloat16)
            decoded[step, rows, :] = kept
            picked = jnp.where(ends == step, kept.astype(jnp.float32), picked)
        at_finish[rows, :] = picked.astype(jnp.bfloat16)

    outgoing[...] = jnp.dot(
        one_hot[...], at_finish[...], preferred_element_type=jnp.float32
    ).astype(jnp.bfloat16)
    for d in range(1, TP):
        to = (tp + d) % TP
        send(
            outgoing.at[pl.ds(pl.multiple_of(to * 16, 16), 16), :],
            stage_one.at[tp],
            one_send,
            one_recv,
            d,
            (rep, to),
        )
    stage_one[tp] = outgoing[pl.ds(pl.multiple_of(tp * 16, 16), 16), :]
    for d in range(1, TP):
        receive(stage_one.at[(tp + TP - d) % TP], one_send, one_recv, d)
    for t in range(TP):
        for part in range(QC // HD):
            arrived[:, t * 4 + part, :] = stage_one[t, :, part * HD : (part + 1) * HD].astype(jnp.float32)
    stage_two[0] = arrived[...].astype(jnp.bfloat16)
    for d in range(1, REP):
        to = (rep + d) % REP
        send(
            stage_two.at[0, pl.ds(to * 2, 2)],
            stage_two.at[1, pl.ds(rep * 2, 2)],
            two_send,
            two_recv,
            d,
            (to, tp),
        )
    stage_two[1, pl.ds(rep * 2, 2)] = stage_two[0, pl.ds(rep * 2, 2)]
    for d in range(1, REP):
        receive(stage_two.at[1, pl.ds((rep + REP - d) % REP * 2, 2)], two_send, two_recv, d)
    for rank in range(2):
        for r in range(REP):
            arrived[rank * REP + r] = stage_two[1, r * 2 + rank].astype(jnp.float32)
    for part in range(D // HD):
        returned[:, part * HD : (part + 1) * HD] = arrived[:, part, :].astype(jnp.bfloat16)

    for copy in pending:
        copy.wait_send()


def per_device(
    hidden,
    norm_gain,
    q_weight,
    k_weight,
    v_weight,
    o_weight,
    key_cache,
    value_cache,
    cache_len,
    finish,
    owner,
):
    positions = cache_len[None, :] + jnp.arange(STEPS, dtype=jnp.int32)[:, None]
    half = HD // 2
    freqs = 500000.0 ** (-(jnp.arange(half, dtype=jnp.float32) * 2.0) / HD)
    angles = (positions.astype(jnp.float32)[..., None] * freqs).reshape(TOKENS, half)
    cosine, sine = jnp.cos(angles), jnp.sin(angles)
    cosine = jnp.concatenate([cosine, cosine], axis=-1)
    sine = jnp.concatenate([-sine, sine], axis=-1)

    owner_flat = owner[:, 0]
    is_returned = finish < STEPS
    row_ids = jnp.arange(ROWS)
    same = (
        (owner_flat[:, None] == owner_flat[None, :])
        & is_returned[None, :]
        & (row_ids[None, :] < row_ids[:, None])
    )
    rank = jnp.sum(same.astype(jnp.int32), axis=1)
    slot = (owner_flat % TP) * (REP * 2) + (owner_flat // TP) * 2 + rank
    slot = jnp.where(is_returned, slot, -1)
    one_hot = (jnp.arange(REP * TP * 2)[:, None] == slot[None, :]).astype(jnp.bfloat16)

    hbm = pl.BlockSpec(memory_space=pl.ANY)
    vmem = pl.BlockSpec(memory_space=pltpu.VMEM)
    smem = pl.BlockSpec(memory_space=pltpu.SMEM)
    dma = pltpu.SemaphoreType.DMA
    bf16, f32 = jnp.bfloat16, jnp.float32
    return pl.pallas_call(
        kernel,
        out_shape=(
            jax.ShapeDtypeStruct((STEPS, ROWS, QC), bf16),
            jax.ShapeDtypeStruct((16, D), bf16),
        ),
        in_specs=[hbm, vmem, hbm, hbm, hbm, hbm, hbm, hbm, smem, vmem, vmem, vmem, vmem],
        out_specs=(vmem, vmem),
        scratch_shapes=[
            pltpu.VMEM((2, CROWS, D), bf16),
            pltpu.VMEM((REP, TOKENS, BLOCK), bf16),
            pltpu.VMEM((REP, BLOCK, WC), bf16),
            pltpu.VMEM((REP * SHARD, D), bf16),
            pltpu.VMEM((ROWS, KEYS, HD), bf16),
            pltpu.VMEM((ROWS, KEYS, HD), bf16),
            pltpu.VMEM((TOKENS, WC), f32),
            pltpu.VMEM((ROWS, 16, HD), f32),
            pltpu.VMEM((2, TOKENS, HD), bf16),
            pltpu.VMEM((CROWS, 16, HD), f32),
            pltpu.VMEM((TP, TOKENS, QC), bf16),
            pltpu.VMEM((TOKENS, QC), f32),
            pltpu.VMEM((STEPS, ROWS, QC), bf16),
            pltpu.VMEM((ROWS, QC), bf16),
            pltpu.VMEM((256, QC), bf16),
            pltpu.VMEM((TP, 16, QC), bf16),
            pltpu.VMEM((ROWS, 16, HD), f32),
            pltpu.VMEM((2, 16, D // HD, HD), bf16),
            pltpu.VMEM((16, D // HD, HD), f32),
            dma((2,)),
            dma((6,)),
            dma((2 * TP,)),
            dma((2 * TP,)),
            dma((18,)),
            dma((18,)),
            dma((18,)),
            dma((18,)),
            dma((1,)),
            dma((1,)),
            dma((18 * CHUNKS,)),
            dma((18 * CHUNKS,)),
            dma((TP,)),
            dma((TP,)),
            dma((REP,)),
            dma((REP,)),
        ],
        compiler_params=pltpu.CompilerParams(
            collective_id=0, has_side_effects=True, vmem_limit_bytes=60 * 1024 * 1024
        ),
    )(
        hidden,
        norm_gain.reshape(1, D),
        q_weight,
        k_weight,
        v_weight,
        o_weight,
        key_cache,
        value_cache,
        cache_len,
        finish.reshape(ROWS, 1),
        cosine,
        sine,
        one_hot,
    )


def solution(mesh):
    placed = (
        P(None, "rep", None),
        P(),
        P(("rep", "tp"), None),
        P(("rep", "tp"), None),
        P(("rep", "tp"), None),
        P(("tp", "rep"), None),
        P("rep", "tp", None, None),
        P("rep", "tp", None, None),
        P("rep"),
        P("rep"),
        P("rep", None),
    )
    return jax.shard_map(
        per_device,
        mesh=mesh,
        in_specs=placed,
        out_specs=(P(None, "rep", "tp"), P(("rep", "tp"), None)),
        check_vma=False,
    )
```

```python
import jax
import jax.numpy as jnp
import numpy as np
from jax import lax
from jax.experimental import pallas as pl
from jax.experimental.pallas import tpu as pltpu
from jax.sharding import PartitionSpec as P

MESH = pl.DeviceIdType.MESH
KV = 8
STEPS = 4
ROWS = 128
HD = 128
CACHE = 192
KEYS = CACHE + 16
D = 8192
REP = 8
TP = 16
QC = 512
WC = QC + HD
SHARD = 64
BLOCK = TP * SHARD
TOKENS = STEPS * ROWS
CHUNKS = 4
SLOTS = 4
CROWS = ROWS // CHUNKS
HALF_ROWS = ROWS // 2
HALF_TOKENS = HALF_ROWS * STEPS
EPS = 1e-05

STAGES = ((0, 384), (384, 256))
OUT_CUT = 5120


def kernel(
    hidden,
    gain,
    q_weight,
    k_weight,
    v_weight,
    o_weight,
    key_cache,
    value_cache,
    lens,
    lens_row,
    finish_row,
    owner,
    frequency,
    decoded,
    returned,
    staged,
    shared,
    normed,
    weights,
    out_rows,
    keys,
    values,
    acc,
    queries,
    partial,
    pair,
    attn_rows,
    gathered,
    out_acc,
    residual,
    cosine,
    sine,
    one_hot,
    ends,
    limits,
    at_finish,
    outgoing,
    stage_one,
    spread,
    stage_two,
    arrived,
    load_sem,
    local_sem,
    a2a_send,
    a2a_recv,
    norm_send,
    norm_recv,
    qkv_send,
    qkv_recv,
    part_send,
    part_recv,
    out_send,
    out_recv,
    pair_send,
    pair_recv,
    attn_send,
    attn_recv,
    one_send,
    one_recv,
    two_send,
    two_recv,
):
    rep = lax.axis_index("rep")
    tp = lax.axis_index("tp")
    y, x = rep // 4, rep % 4
    across = (1 - y) * 4
    mine = y * 4
    east, west, far = (x + 1) % 4, (x + 3) % 4, (x + 2) % 4
    rep_east, rep_west, rep_y = mine + east, mine + west, across + x
    z, low = tp // 4, tp % 4
    core_peer = tp + 1 - 2 * (tp % 2)
    hi_peer = tp + 2 - 4 * ((tp // 2) % 2)
    pending = []

    def send(src, dst, sends, recvs, k, to):
        copy = pltpu.make_async_remote_copy(
            src_ref=src,
            dst_ref=dst,
            send_sem=sends.at[k],
            recv_sem=recvs.at[k],
            device_id=to,
            device_id_type=MESH,
        )
        copy.start()
        pending.append(copy)

    def receive(region, sends, recvs, k):
        pltpu.make_async_remote_copy(
            src_ref=region,
            dst_ref=region,
            send_sem=sends.at[k],
            recv_sem=recvs.at[k],
            device_id=(rep, core_peer),
            device_id_type=MESH,
        ).wait_recv()

    barrier = pltpu.get_barrier_semaphore()
    for d in range(1, TP):
        pl.semaphore_signal(
            barrier, inc=1, device_id=(rep, (tp + d) % TP), device_id_type=MESH
        )
    for d in range(1, REP):
        pl.semaphore_signal(
            barrier, inc=1, device_id=((rep + d) % REP, tp), device_id_type=MESH
        )
    key_load = pltpu.make_async_copy(
        key_cache.at[:, 0], keys.at[:, pl.ds(0, CACHE), :], local_sem.at[0]
    )
    value_load = pltpu.make_async_copy(
        value_cache.at[:, 0], values.at[:, pl.ds(0, CACHE), :], local_sem.at[1]
    )
    my_cols = pl.ds(pl.multiple_of(tp * QC, QC), QC)
    residual_load = pltpu.make_async_copy(
        hidden.at[:, :, my_cols], residual, local_sem.at[2]
    )
    my_rows = pl.ds(pl.multiple_of(tp * SHARD, SHARD), SHARD)
    q_load = pltpu.make_async_copy(
        q_weight.at[:, my_cols], weights.at[x, my_rows, pl.ds(HD, QC)], local_sem.at[3]
    )
    kv_cols = pl.ds(pl.multiple_of((tp // 2) * HD, HD), HD)
    my_kv = weights.at[x, my_rows, pl.ds(0, HD)]
    k_load = pltpu.make_async_copy(k_weight.at[:, kv_cols], my_kv, local_sem.at[4])
    v_load = pltpu.make_async_copy(v_weight.at[:, kv_cols], my_kv, local_sem.at[4])

    def out_block(r, part):
        start, size = {
            "A": (0, OUT_CUT),
            "A0": (0, OUT_CUT // 2),
            "A1": (OUT_CUT // 2, OUT_CUT // 2),
            "B": (OUT_CUT, D - OUT_CUT),
            "B0": (OUT_CUT, (D - OUT_CUT) // 2),
            "B1": (OUT_CUT + (D - OUT_CUT) // 2, (D - OUT_CUT) // 2),
            "all": (0, D),
        }[part]
        return out_rows.at[
            pl.ds(pl.multiple_of(r * SHARD, SHARD), SHARD), pl.ds(start, size)
        ]

    out_load = pltpu.make_async_copy(o_weight, out_block(rep, "all"), local_sem.at[5])
    q_load.start()
    pl.when(tp % 2 == 0)(k_load.start)
    pl.when(tp % 2 == 1)(v_load.start)
    out_load.start()

    def hidden_load(step, slot):
        return pltpu.make_async_copy(
            hidden.at[step // CHUNKS, pl.ds(pl.multiple_of((step % CHUNKS) * CROWS, CROWS), CROWS), :],
            staged.at[slot],
            load_sem.at[slot],
        )

    hidden_load(tp, SLOTS).start()
    for step in range(SLOTS - 1):
        hidden_load(step, step).start()
    def norm_rows(slot, half, part, store):
        part_rows = pl.ds(pl.multiple_of(part * 16, 16), 16)
        values_f = staged[slot, part_rows, :].astype(jnp.float32)
        mean = jnp.mean(values_f * values_f, axis=-1, keepdims=True)
        scale = lax.rsqrt(mean + EPS)
        for b in range(4):
            cols = pl.ds(pl.multiple_of(half * (D // 2) + b * BLOCK, BLOCK), BLOCK)
            block = staged[slot, part_rows, cols].astype(jnp.float32)
            block = block * scale * gain[:, cols].astype(jnp.float32)
            store(b, block.astype(jnp.bfloat16))

    def norm_step(step, carry):
        slot = step % SLOTS
        hidden_load(step, slot).wait()

        @pl.when(step + SLOTS - 1 < STEPS * CHUNKS)
        def _():
            hidden_load(step + SLOTS - 1, (step + SLOTS - 1) % SLOTS).start()

        def sixteen(part, carry):
            rows = pl.ds(pl.multiple_of(step * CROWS + part * 16, 16), 16)

            def store(b, block):
                normed[0, b, rows, :] = block

            norm_rows(slot, y, part, store)
            return carry

        return lax.fori_loop(0, CROWS // 16, sixteen, carry)

    with jax.named_scope("norm_shared"):
        hidden_load(tp, SLOTS).wait()

        def sixteen_shared(part, carry):
            rows = pl.ds(pl.multiple_of(part * 16, 16), 16)

            def store(b, block):
                shared[b, rows, :] = block

            norm_rows(SLOTS, 1 - y, part, store)
            return carry

        lax.fori_loop(0, CROWS // 16, sixteen_shared, 0)

    def norm_block(t, part):
        start, size = {"all": (0, 4), "0": (0, 2), "1": (2, 2)}[part]
        rows = pl.ds(pl.multiple_of(t * CROWS, CROWS), CROWS)
        return normed.at[1, pl.ds(start, size), rows, :]

    with jax.named_scope("greet"):
        pl.semaphore_wait(barrier, TP - 1 + REP - 1)

    q_parts = ((0, STAGES[0][1] - HD), (STAGES[0][1] - HD, STAGES[1][1]))
    def a2a_go(stage):
        start, size = q_parts[stage]
        for d in range(1, TP):
            to = (tp + d) % TP
            there = (rep, to)
            send(
                q_weight.at[:, pl.ds(pl.multiple_of(to * QC + start, HD), size)],
                weights.at[x, my_rows, pl.ds(HD + start, size)],
                a2a_send,
                a2a_recv,
                (1 + stage) * TP + d,
                there,
            )
            if stage == 1:
                continue
            cols = pl.ds(pl.multiple_of((to // 2) * HD, HD), HD)

            def kv_copy(source, cols=cols, d=d, there=there):
                return pltpu.make_async_remote_copy(
                    src_ref=source.at[:, cols],
                    dst_ref=weights.at[x, my_rows, pl.ds(0, HD)],
                    send_sem=a2a_send.at[d],
                    recv_sem=a2a_recv.at[d],
                    device_id=there,
                    device_id_type=MESH,
                )

            from_k, from_v = kv_copy(k_weight), kv_copy(v_weight)
            pl.when(to % 2 == 0)(from_k.start)
            pl.when(to % 2 == 1)(from_v.start)
            pending.append(from_k)

    def a2a_got(stage):
        start, size = q_parts[stage]
        for d in range(1, TP):
            source = (tp + TP - d) % TP
            rows = pl.ds(pl.multiple_of(source * SHARD, SHARD), SHARD)
            receive(weights.at[x, rows, pl.ds(HD + start, size)], a2a_send, a2a_recv, (1 + stage) * TP + d)
            if stage == 0:
                receive(weights.at[x, rows, pl.ds(0, HD)], a2a_send, a2a_recv, d)

    east_dev, west_dev, y_dev = (rep_east, tp), (rep_west, tp), (rep_y, tp)

    def o_go(k, r, part, to, src=None):
        dst = out_block(r, part)
        send(dst if src is None else src, dst, out_send, out_recv, k, to)

    def o_got(k, r, part):
        receive(out_block(r, part), out_send, out_recv, k)

    o_a = o_weight.at[:, pl.ds(0, OUT_CUT)]
    o_b = o_weight.at[:, pl.ds(OUT_CUT, D - OUT_CUT)]

    z_up, z_down, z_far = (z + 1) % 4 * 4, (z + 3) % 4 * 4, (z + 2) % 4 * 4
    low_hi, low_core = hi_peer % 4, core_peer % 4
    low_both = low_hi + 1 - 2 * (low_hi % 2)
    up_dev, down_dev = (rep, z_up + low), (rep, z_down + low)
    hi_dev, core_dev = (rep, hi_peer), (rep, core_peer)

    class TpGather:
        def __init__(self, block, sends, recvs, base):
            self.block, self.sends, self.recvs, self.base = block, sends, recvs, base

        def go(self, k, t, to, part="all"):
            block = self.block(t, part)
            send(block, block, self.sends, self.recvs, self.base + k, to)

        def got(self, k, t, part="all"):
            receive(self.block(t, part), self.sends, self.recvs, self.base + k)

        def first(self):
            self.go(0, tp, hi_dev)
            self.go(1, tp, up_dev)
            self.go(2, tp, down_dev)
            self.go(3, tp, core_dev)

        def second(self):
            self.got(0, hi_peer)
            self.go(4, hi_peer, up_dev)
            self.go(5, hi_peer, down_dev)
            self.got(1, z_down + low)
            self.go(7, z_down + low, up_dev, "0")
            self.got(2, z_up + low)
            self.go(8, z_up + low, down_dev, "1")
            self.go(6, hi_peer, core_dev)
            self.go(9, z_down + low, core_dev)
            self.go(10, z_up + low, core_dev)

        def third(self):
            self.got(4, z_down + low_hi)
            self.go(11, z_down + low_hi, up_dev, "0")
            self.got(5, z_up + low_hi)
            self.go(12, z_up + low_hi, down_dev, "1")
            self.go(13, z_down + low_hi, core_dev)
            self.go(14, z_up + low_hi, core_dev)
            self.got(7, z_far + low, "0")
            self.got(8, z_far + low, "1")
            self.go(15, z_far + low, core_dev)

        def fourth(self):
            self.got(11, z_far + low_hi, "0")
            self.got(12, z_far + low_hi, "1")
            self.go(16, z_far + low_hi, core_dev)

        def near(self):
            self.got(3, core_peer)
            self.got(6, z * 4 + low_both)
            self.got(9, z_down + low_core)
            self.got(10, z_up + low_core)
            self.got(13, z_down + low_both)
            self.got(14, z_up + low_both)

        def rest(self):
            self.got(15, z_far + low_core)
            self.got(16, z_far + low_both)

    norm_gather = TpGather(norm_block, norm_send, norm_recv, 0)
    send(shared, norm_block(tp, "all"), norm_send, norm_recv, 17, y_dev)
    a2a_go(0)
    a2a_go(1)
    o_go(9, rep, "B", east_dev, o_b)
    o_go(10, rep, "B", west_dev, o_b)

    with jax.named_scope("tables"):
        square = (ROWS, ROWS)
        rows_at = lax.broadcasted_iota(jnp.int32, square, 0)
        cols_at = lax.broadcasted_iota(jnp.int32, square, 1)

        def flip(values):
            return values.astype(jnp.float32).T.astype(jnp.int32)

        lens_col = jnp.broadcast_to(lens_row[...].astype(jnp.float32).reshape(1, ROWS), square).T
        finish_cols = jnp.broadcast_to(finish_row[...].reshape(1, ROWS), square)
        finish_rows = flip(finish_cols)
        ends[...] = finish_rows
        owner_rows = jnp.broadcast_to(owner[...], square)
        owner_cols = flip(owner_rows)
        sign = jnp.where(cols_at < HD // 2, -1.0, 1.0)
        for step in range(STEPS):
            angles = (lens_col + float(step)) * frequency[...]
            cosine[pl.ds(step * ROWS, ROWS), :] = jnp.cos(angles)
            sine[pl.ds(step * ROWS, ROWS), :] = jnp.sin(angles) * sign
        same = (owner_rows == owner_cols) & (finish_rows < STEPS) & (rows_at < cols_at)
        rank = jnp.sum(jnp.where(same, 1.0, 0.0), axis=0, keepdims=True).astype(jnp.int32)
        owner_row = owner_cols[0:1, :]
        slot = (owner_row % TP) * (REP * 2) + (owner_row // TP) * 2 + rank
        slot = jnp.where(finish_cols[0:1, :] < STEPS, slot, -1)
        slots_at = lax.broadcasted_iota(jnp.int32, (REP * TP * 2, ROWS), 0)
        one_hot[...] = jnp.where(slots_at == slot, 1.0, 0.0).astype(jnp.bfloat16)
        key_at = lax.broadcasted_iota(jnp.int32, (KEYS, HD), 0)
        step_at = lax.broadcasted_iota(jnp.int32, (KEYS, HD), 1) % 8 // 2
        new_at = jnp.where(key_at - CACHE <= step_at, -1, 4 * CACHE)
        limits[...] = jnp.where(key_at < CACHE, key_at, new_at)

    def ring_block(stage, b, half):
        start, size = STAGES[stage]
        return weights.at[b, pl.ds(half * (BLOCK // 2), BLOCK // 2), pl.ds(start, size)]

    def w_go(stage, k, b, half, to):
        block = ring_block(stage, b, half)
        send(block, block, qkv_send, qkv_recv, stage * 6 + k, to)

    def w_got(stage, k, b, half):
        receive(ring_block(stage, b, half), qkv_send, qkv_recv, stage * 6 + k)

    def ring_own(stage):
        w_go(stage, 0, x, 0, east_dev)
        w_go(stage, 1, x, 1, west_dev)
        w_go(stage, 2, x, 1, east_dev)
        w_go(stage, 3, x, 0, west_dev)

    def ring_on(stage):
        w_got(stage, 0, west, 0)
        w_go(stage, 4, west, 0, east_dev)
        w_got(stage, 1, east, 1)
        w_go(stage, 5, east, 1, west_dev)

    def ring_near(stage):
        w_got(stage, 2, west, 1)
        w_got(stage, 3, east, 0)

    def ring_far(stage):
        w_got(stage, 4, far, 0)
        w_got(stage, 5, far, 1)

    def project(stage, which, b, first=False):
        start, size = STAGES[stage]

        def tile(m, carry):
            rows = pl.ds(pl.multiple_of(m * 256, 256), 256)
            part = jnp.dot(
                normed[which, b, rows, :],
                weights[b, :, start : start + size],
                preferred_element_type=jnp.float32,
            )
            if first:
                acc[which, rows, start : start + size] = part
            else:
                acc[which, rows, start : start + size] += part
            return carry

        lax.fori_loop(0, TOKENS // 256, tile, 0)

    def part_block(which, stage):
        start, size = STAGES[stage]
        return partial.at[which, :, pl.ds(start, size)]

    def part_go(stage):
        start, size = STAGES[stage]
        partial[0, :, start : start + size] = acc[1, :, start : start + size].astype(jnp.bfloat16)
        send(part_block(0, stage), part_block(1, stage), part_send, part_recv, stage, y_dev)

    def part_got(stage):
        receive(part_block(1, stage), part_send, part_recv, stage)

    with jax.named_scope("norm_over_y"):
        receive(norm_block(tp, "all"), norm_send, norm_recv, 17)
        norm_gather.first()
    with jax.named_scope("a2a_wait"):
        q_load.wait()
        k_load.wait()
        a2a_got(0)
        ring_own(0)
        o_go(0, rep, "A", y_dev, o_a)
    with jax.named_scope("norm"):
        lax.fori_loop(0, 8, norm_step, 0)
    with jax.named_scope("norm_second"):
        norm_gather.second()
    with jax.named_scope("ring_on_0"):
        ring_on(0)
    with jax.named_scope("norm"):
        lax.fori_loop(8, 16, norm_step, 0)
    with jax.named_scope("ring_near_0"):
        ring_near(0)
        a2a_got(1)
        ring_own(1)
    with jax.named_scope("norm_third"):
        norm_gather.third()
    key_load.start()
    value_load.start()
    residual_load.start()
    with jax.named_scope("project"):
        project(0, 0, x, True)
        project(0, 0, west)
        project(0, 0, east)
    with jax.named_scope("norm_last"):
        norm_gather.fourth()
        norm_gather.near()
        norm_gather.rest()
    with jax.named_scope("project"):
        project(0, 1, x, True)
        project(0, 1, west)
        project(0, 1, east)
    with jax.named_scope("ring_far_0"):
        ring_far(0)
        project(0, 1, far)
        part_go(0)
        o_go(11, rep, "B", y_dev, o_b)
        o_got(9, mine + west, "B")
        o_got(10, mine + east, "B")
        project(0, 0, far)
    with jax.named_scope("ring_on_1"):
        ring_on(1)
    with jax.named_scope("project"):
        project(1, 0, x, True)
        project(1, 1, x, True)
    with jax.named_scope("out_first"):
        o_go(1, rep, "A", east_dev, o_a)
        o_go(2, rep, "A", west_dev, o_a)
        o_go(12, mine + west, "B0", east_dev)
        o_go(13, mine + east, "B1", west_dev)

    def rotate(block, rows):
        return block * cosine[rows, :] + pltpu.roll(block, HD // 2, 1) * sine[rows, :]

    def total(step, start):
        rows = pl.ds(step * ROWS, ROWS)
        cols = slice(start, start + HD)
        return acc[0, rows, cols] + partial[1, rows, cols].astype(jnp.float32)

    def place_queries(stage):
        for step in range(STEPS):
            rows = pl.ds(step * ROWS, ROWS)
            for h in range(2):
                start = HD + (stage * 2 + h) * HD
                queries[stage, :, step * 2 + h, :] = rotate(total(step, start), rows)

    is_key = tp % 2 == 0
    with jax.named_scope("keys"):
        part_got(0)
        for step in range(STEPS):
            rows = pl.ds(step * ROWS, ROWS)
            block = total(step, 0)
            pair[0, rows, :] = jnp.where(is_key, rotate(block, rows), block).astype(jnp.bfloat16)
        send(pair.at[0], pair.at[1], pair_send, pair_recv, 0, core_dev)
        place_queries(0)
    with jax.named_scope("ring_near_1"):
        ring_near(1)
    with jax.named_scope("project"):
        project(1, 1, west)
        project(1, 1, east)
        project(1, 0, west)
        project(1, 0, east)
    receive(pair.at[1], pair_send, pair_recv, 0)
    key_load.wait()
    value_load.wait()
    zeros = jnp.zeros((ROWS, 16, HD), jnp.float32)
    for place, target in ((0, keys), (1, values)):
        spread[...] = zeros
        slot = (tp + place) % 2
        for step in range(STEPS):
            spread[:, step, :] = pair[slot, pl.ds(step * ROWS, ROWS), :].astype(jnp.float32)
        target[:, pl.ds(CACHE, 16), :] = spread[...].astype(jnp.bfloat16)

    row_of = lax.broadcasted_iota(jnp.int32, (KEYS, HD), 1) // 8
    score_scale = 1.0 / (float(HD) ** 0.5)

    def attend(stage, half):
        def rows_of_16(it, carry):
            first = half * HALF_ROWS + it * 16
            query = queries[stage, pl.ds(first, 16)].reshape(16 * 8, HD).astype(jnp.bfloat16)
            scores = None
            valid = jnp.zeros((1, HD), jnp.int32)
            for u in range(16):
                part = lax.dot_general(
                    keys[first + u], query, (((1,), (1,)), ((), ())), preferred_element_type=jnp.float32
                )
                scores = part if scores is None else jnp.where(row_of == u, part, scores)
                valid = jnp.where(row_of[0:1, :] == u, lens[first + u], valid)
            scores = jnp.where(limits[...] < valid, scores, -1e30)
            top = jnp.max(scores, axis=0, keepdims=True)
            weight = jnp.exp((scores - top) * score_scale)
            total = jnp.sum(weight, axis=0, keepdims=True)
            probs = (weight * (1.0 / total)).T
            for u in range(16):
                attn_rows[it * 16 + u] = jnp.dot(
                    probs[u * 8 : (u + 1) * 8].astype(jnp.bfloat16),
                    values[first + u],
                    preferred_element_type=jnp.float32,
                )
            return carry

        lax.fori_loop(0, HALF_ROWS // 16, rows_of_16, 0)
        for step in range(STEPS):
            for h in range(2):
                gathered[
                    tp,
                    pl.ds(half * HALF_TOKENS + step * HALF_ROWS, HALF_ROWS),
                    pl.ds((stage * 2 + h) * HD, HD),
                ] = attn_rows[:, step * 2 + h, :].astype(jnp.bfloat16)

    def attn_block(t, chunk, part="all"):
        size = HALF_TOKENS // 2
        start, size = {"all": (0, HALF_TOKENS), "0": (0, size), "1": (size, size)}[part]
        rows = pl.ds(chunk % 2 * HALF_TOKENS + start, size)
        return gathered.at[t, rows, pl.ds(chunk // 2 * 2 * HD, 2 * HD)]

    PER = 18
    gathers = [
        TpGather(
            lambda t, part, chunk=chunk: attn_block(t, chunk, part), attn_send, attn_recv, chunk * PER
        )
        for chunk in range(CHUNKS)
    ]

    def attend_and_send(chunk):
        with jax.named_scope("attend"):
            attend(chunk // 2, chunk % 2)
        gathers[chunk].first()

    attend_and_send(0)
    with jax.named_scope("ring_far_1"):
        ring_far(1)
        project(1, 1, far)
        part_go(1)
        project(1, 0, far)
        o_go(14, mine + west, "B", y_dev)
    with jax.named_scope("out_second"):
        o_got(0, rep_y, "A")
        o_go(3, rep_y, "A", east_dev)
        o_go(4, rep_y, "A", west_dev)
    attend_and_send(1)
    with jax.named_scope("attn_a"):
        gathers[0].second()
    with jax.named_scope("queries"):
        part_got(1)
        place_queries(1)
    attend_and_send(2)
    o_go(15, mine + east, "B", y_dev)
    with jax.named_scope("attn_b"):
        gathers[1].second()
    with jax.named_scope("out_third"):
        o_got(1, mine + west, "A")
        o_go(5, mine + west, "A0", east_dev)
        o_got(2, mine + east, "A")
        o_go(6, mine + east, "A1", west_dev)
    attend_and_send(3)
    with jax.named_scope("out_fourth"):
        o_got(12, mine + far, "B0")
        o_go(16, mine + far, "B0", y_dev)
        o_got(13, mine + far, "B1")
        o_go(17, mine + far, "B1", y_dev)
    with jax.named_scope("attn_c"):
        gathers[0].third()
        gathers[2].second()
    with jax.named_scope("out_fifth"):
        o_got(3, across + west, "A")
        o_go(7, across + west, "A0", east_dev)
        o_got(4, across + east, "A")
        o_go(8, across + east, "A1", west_dev)
    with jax.named_scope("attn_d"):
        gathers[1].third()
        gathers[0].fourth()
        gathers[3].second()
    with jax.named_scope("attn_e"):
        gathers[2].third()
        gathers[1].fourth()
    with jax.named_scope("attn_f"):
        gathers[3].third()
    with jax.named_scope("out_last"):
        out_load.wait()
        o_got(11, rep_y, "B")
        o_got(14, across + west, "B")
        o_got(15, across + east, "B")
        o_got(5, mine + far, "A0")
        o_got(6, mine + far, "A1")
        o_got(16, across + far, "B0")
        o_got(17, across + far, "B1")
        o_got(7, across + far, "A0")
        o_got(8, across + far, "A1")
    out_acc[...] = jnp.zeros_like(out_acc)

    def out_product(first):
        def step(t, carry):
            cols = pl.ds(pl.multiple_of((first + t) * QC, QC), QC)
            out_acc[...] += lax.dot_general(
                gathered[first + t],
                out_rows[:, cols],
                (((1,), (1,)), ((), ())),
                preferred_element_type=jnp.float32,
            )
            return carry

        lax.fori_loop(0, 4, step, 0)

    with jax.named_scope("attn_g"):
        for gather in gathers:
            gather.near()
    with jax.named_scope("out_product"):
        out_product(z * 4)
        out_product(z_down)
        out_product(z_up)
    with jax.named_scope("attn_h"):
        gathers[2].fourth()
        gathers[3].fourth()
        for gather in gathers:
            gather.rest()
    with jax.named_scope("out_product"):
        out_product(z_far)

    residual_load.wait()
    for half in range(2):
        rows = pl.ds(half * HALF_ROWS, HALF_ROWS)
        ended = ends[rows, 0:1]
        picked = jnp.zeros((HALF_ROWS, QC), jnp.float32)
        for step in range(STEPS):
            total = out_acc[pl.ds(half * HALF_TOKENS + step * HALF_ROWS, HALF_ROWS), :]
            total = total + residual[step, rows, :].astype(jnp.float32)
            kept = jnp.where(ended >= step, total, 0.0).astype(jnp.bfloat16)
            decoded[step, rows, :] = kept
            picked = jnp.where(ended == step, kept.astype(jnp.float32), picked)
        at_finish[rows, :] = picked.astype(jnp.bfloat16)

    outgoing[...] = jnp.dot(
        one_hot[...], at_finish[...], preferred_element_type=jnp.float32
    ).astype(jnp.bfloat16)
    for d in range(1, TP):
        to = (tp + d) % TP
        send(
            outgoing.at[pl.ds(pl.multiple_of(to * 16, 16), 16), :],
            stage_one.at[tp],
            one_send,
            one_recv,
            d,
            (rep, to),
        )
    stage_one[tp] = outgoing[pl.ds(pl.multiple_of(tp * 16, 16), 16), :]
    with jax.named_scope("ended_one"):
        for d in range(1, TP):
            receive(stage_one.at[(tp + TP - d) % TP], one_send, one_recv, d)
    for t in range(TP):
        for part in range(QC // HD):
            arrived[:, t * 4 + part, :] = stage_one[t, :, part * HD : (part + 1) * HD].astype(jnp.float32)
    stage_two[0] = arrived[...].astype(jnp.bfloat16)
    for d in range(1, REP):
        to = (rep + d) % REP
        send(
            stage_two.at[0, pl.ds(to * 2, 2)],
            stage_two.at[1, pl.ds(rep * 2, 2)],
            two_send,
            two_recv,
            d,
            (to, tp),
        )
    stage_two[1, pl.ds(rep * 2, 2)] = stage_two[0, pl.ds(rep * 2, 2)]
    with jax.named_scope("ended_two"):
        for d in range(1, REP):
            receive(stage_two.at[1, pl.ds((rep + REP - d) % REP * 2, 2)], two_send, two_recv, d)
    for rank in range(2):
        for r in range(REP):
            arrived[rank * REP + r] = stage_two[1, r * 2 + rank].astype(jnp.float32)
    for part in range(D // HD):
        returned[:, part * HD : (part + 1) * HD] = arrived[:, part, :].astype(jnp.bfloat16)

    with jax.named_scope("sends"):
        for copy in pending:
            copy.wait_send()


def per_device(
    hidden,
    norm_gain,
    q_weight,
    k_weight,
    v_weight,
    o_weight,
    key_cache,
    value_cache,
    cache_len,
    finish,
    owner,
):
    half = HD // 2
    frequency = 500000.0 ** (-(np.arange(HD) % half * 2.0) / HD)
    frequency = jnp.asarray(frequency.reshape(1, HD), jnp.float32)
    hbm = pl.BlockSpec(memory_space=pl.ANY)
    vmem = pl.BlockSpec(memory_space=pltpu.VMEM)
    smem = pl.BlockSpec(memory_space=pltpu.SMEM)
    dma = pltpu.SemaphoreType.DMA
    bf16, f32 = jnp.bfloat16, jnp.float32
    return pl.pallas_call(
        kernel,
        out_shape=(
            jax.ShapeDtypeStruct((STEPS, ROWS, QC), bf16),
            jax.ShapeDtypeStruct((16, D), bf16),
        ),
        in_specs=[hbm, vmem, hbm, hbm, hbm, hbm, hbm, hbm, smem, vmem, vmem, vmem, vmem],
        out_specs=(vmem, vmem),
        scratch_shapes=[
            pltpu.VMEM((SLOTS + 1, CROWS, D), bf16),
            pltpu.VMEM((4, CROWS, BLOCK), bf16),
            pltpu.VMEM((2, 4, TOKENS, BLOCK), bf16),
            pltpu.VMEM((4, BLOCK, WC), bf16),
            pltpu.VMEM((REP * SHARD, D), bf16),
            pltpu.VMEM((ROWS, KEYS, HD), bf16),
            pltpu.VMEM((ROWS, KEYS, HD), bf16),
            pltpu.VMEM((2, TOKENS, WC), f32),
            pltpu.VMEM((2, ROWS, 8, HD), f32),
            pltpu.VMEM((2, TOKENS, WC), bf16),
            pltpu.VMEM((2, TOKENS, HD), bf16),
            pltpu.VMEM((HALF_ROWS, 8, HD), f32),
            pltpu.VMEM((TP, TOKENS, QC), bf16),
            pltpu.VMEM((TOKENS, QC), f32),
            pltpu.VMEM((STEPS, ROWS, QC), bf16),
            pltpu.VMEM((TOKENS, HD), f32),
            pltpu.VMEM((TOKENS, HD), f32),
            pltpu.VMEM((REP * TP * 2, ROWS), bf16),
            pltpu.VMEM((ROWS, ROWS), jnp.int32),
            pltpu.VMEM((KEYS, HD), jnp.int32),
            pltpu.VMEM((ROWS, QC), bf16),
            pltpu.VMEM((256, QC), bf16),
            pltpu.VMEM((TP, 16, QC), bf16),
            pltpu.VMEM((ROWS, 16, HD), f32),
            pltpu.VMEM((2, 16, D // HD, HD), bf16),
            pltpu.VMEM((16, D // HD, HD), f32),
            dma((SLOTS + 1,)),
            dma((6,)),
            dma((3 * TP,)),
            dma((3 * TP,)),
            dma((18,)),
            dma((18,)),
            dma((12,)),
            dma((12,)),
            dma((2,)),
            dma((2,)),
            dma((18,)),
            dma((18,)),
            dma((1,)),
            dma((1,)),
            dma((18 * CHUNKS,)),
            dma((18 * CHUNKS,)),
            dma((TP,)),
            dma((TP,)),
            dma((REP,)),
            dma((REP,)),
        ],
        compiler_params=pltpu.CompilerParams(
            collective_id=0, has_side_effects=True, vmem_limit_bytes=60 * 1024 * 1024
        ),
    )(
        hidden,
        norm_gain.reshape(1, D),
        q_weight,
        k_weight,
        v_weight,
        o_weight,
        key_cache,
        value_cache,
        cache_len,
        cache_len,
        finish,
        owner,
        frequency,
    )


def solution(mesh):
    placed = (
        P(None, "rep", None),
        P(),
        P(("rep", "tp"), None),
        P(("rep", "tp"), None),
        P(("rep", "tp"), None),
        P(("tp", "rep"), None),
        P("rep", "tp", None, None),
        P("rep", "tp", None, None),
        P("rep"),
        P("rep"),
        P("rep", None),
    )
    return jax.shard_map(
        per_device,
        mesh=mesh,
        in_specs=placed,
        out_specs=(P(None, "rep", "tp"), P(("rep", "tp"), None)),
        check_vma=False,
    )
```

```python
import jax
import jax.numpy as jnp
import numpy as np
from jax import lax
from jax.experimental import pallas as pl
from jax.experimental.pallas import tpu as pltpu
from jax.sharding import PartitionSpec as P

MESH = pl.DeviceIdType.MESH
KV = 8
STEPS = 4
ROWS = 128
HD = 128
CACHE = 192
KEYS = CACHE + 16
D = 8192
REP = 8
TP = 16
QC = 512
WC = QC + HD
SHARD = 64
BLOCK = TP * SHARD
TOKENS = STEPS * ROWS
CHUNKS = 4
Z_FIRST = ()
SLOTS = 4
CROWS = ROWS // CHUNKS
HALF_ROWS = ROWS // 2
HALF_TOKENS = HALF_ROWS * STEPS
EPS = 1e-05

STAGES = ((0, 384), (384, 256))


def kernel(
    hidden,
    gain,
    q_weight,
    k_weight,
    v_weight,
    o_weight,
    key_cache,
    value_cache,
    lens,
    lens_row,
    finish_row,
    owner,
    frequency,
    decoded,
    returned,
    staged,
    gain_row,
    shared,
    normed,
    weights,
    out_rows,
    keys,
    values,
    acc,
    queries,
    partial,
    pair,
    attn_rows,
    away,
    gathered,
    out_acc,
    out_part,
    residual,
    cosine,
    sine,
    one_hot,
    ends,
    limits,
    at_finish,
    outgoing,
    stage_one,
    spread,
    stage_two,
    arrived,
    load_sem,
    local_sem,
    out_sem,
    a2a_send,
    a2a_recv,
    norm_send,
    norm_recv,
    qkv_send,
    qkv_recv,
    part_send,
    part_recv,
    out_send,
    out_recv,
    pair_send,
    pair_recv,
    away_send,
    away_recv,
    attn_send,
    attn_recv,
    last_send,
    last_recv,
    one_send,
    one_recv,
    two_send,
    two_recv,
):
    rep = lax.axis_index("rep")
    tp = lax.axis_index("tp")
    y, x = rep // 4, rep % 4
    east, west, far = (x + 1) % 4, (x + 3) % 4, (x + 2) % 4
    rep_east, rep_west, rep_y = y * 4 + east, y * 4 + west, (1 - y) * 4 + x
    z, low = tp // 4, tp % 4
    core_peer = tp + 1 - 2 * (tp % 2)
    hi_peer = tp + 2 - 4 * ((tp // 2) % 2)
    pending = []

    def send(src, dst, sends, recvs, k, to, start=True):
        copy = pltpu.make_async_remote_copy(
            src_ref=src,
            dst_ref=dst,
            send_sem=sends.at[k],
            recv_sem=recvs.at[k],
            device_id=to,
            device_id_type=MESH,
        )
        if start:
            copy.start()
        pending.append(copy)
        return copy

    def receive(region, sends, recvs, k):
        pltpu.make_async_remote_copy(
            src_ref=region,
            dst_ref=region,
            send_sem=sends.at[k],
            recv_sem=recvs.at[k],
            device_id=(rep, core_peer),
            device_id_type=MESH,
        ).wait_recv()

    barrier = pltpu.get_barrier_semaphore()
    for d in range(1, TP):
        pl.semaphore_signal(
            barrier, inc=1, device_id=(rep, (tp + d) % TP), device_id_type=MESH
        )
    for d in range(1, REP):
        pl.semaphore_signal(
            barrier, inc=1, device_id=((rep + d) % REP, tp), device_id_type=MESH
        )
    both_peer = hi_peer + 1 - 2 * (tp % 2)
    for peer in (core_peer, both_peer):
        pl.semaphore_signal(barrier, inc=1, device_id=(rep_y, peer), device_id_type=MESH)
    key_load = pltpu.make_async_copy(
        key_cache.at[:, 0], keys.at[:, pl.ds(0, CACHE), :], local_sem.at[0]
    )
    value_load = pltpu.make_async_copy(
        value_cache.at[:, 0], values.at[:, pl.ds(0, CACHE), :], local_sem.at[1]
    )
    my_cols = pl.ds(pl.multiple_of(tp * QC, QC), QC)
    residual_load = pltpu.make_async_copy(
        hidden.at[:, :, my_cols], residual, local_sem.at[2]
    )
    my_rows = pl.ds(pl.multiple_of(tp * SHARD, SHARD), SHARD)
    q_load = pltpu.make_async_copy(
        q_weight.at[:, my_cols], weights.at[x, my_rows, pl.ds(HD, QC)], local_sem.at[3]
    )
    kv_cols = pl.ds(pl.multiple_of((tp // 2) * HD, HD), HD)
    my_kv = weights.at[x, my_rows, pl.ds(0, HD)]
    k_load = pltpu.make_async_copy(k_weight.at[:, kv_cols], my_kv, local_sem.at[4])
    v_load = pltpu.make_async_copy(v_weight.at[:, kv_cols], my_kv, local_sem.at[4])

    def out_block(side, at, part="all"):
        start, size = {"all": (0, D // 2), "0": (0, D // 4), "1": (D // 4, D // 4)}[part]
        rows = pl.ds(pl.multiple_of((side * 4 + at) * SHARD, SHARD), SHARD)
        return out_rows.at[rows, pl.ds(start, size)]

    def out_piece(side, j):
        rows = pl.ds(pl.multiple_of((side * 4 + x) * SHARD, SHARD), SHARD)
        return out_rows.at[rows, pl.ds(j * QC, QC)]

    def out_source(core, j):
        return o_weight.at[:, pl.ds(pl.multiple_of((j * 2 + core) * QC, QC), QC)]

    out_loads = [
        pltpu.make_async_copy(out_source(y, j), out_piece(y, j), out_sem.at[j]) for j in range(TP // 2)
    ]
    q_load.start()
    pl.when(tp % 2 == 0)(k_load.start)
    pl.when(tp % 2 == 1)(v_load.start)
    for load in out_loads:
        load.start()

    def hidden_load(step, slot):
        return pltpu.make_async_copy(
            hidden.at[step // CHUNKS, pl.ds(pl.multiple_of((step % CHUNKS) * CROWS, CROWS), CROWS), :],
            staged.at[slot],
            load_sem.at[slot],
        )

    hidden_load(tp, SLOTS).start()
    gain_row[...] = gain[...].astype(jnp.float32).reshape(1, D)
    for step in range(SLOTS - 1):
        hidden_load(step, step).start()
    def norm_rows(slot, half, part, store):
        part_rows = pl.ds(pl.multiple_of(part * 16, 16), 16)
        values_f = staged[slot, part_rows, :].astype(jnp.float32)
        mean = jnp.mean(values_f * values_f, axis=-1, keepdims=True)
        scale = lax.rsqrt(mean + EPS)
        for b in range(4):
            cols = pl.ds(pl.multiple_of(half * (D // 2) + b * BLOCK, BLOCK), BLOCK)
            block = staged[slot, part_rows, cols].astype(jnp.float32)
            block = block * scale * gain_row[:, cols]
            store(b, block.astype(jnp.bfloat16))

    def norm_step(step, carry):
        slot = step % SLOTS
        hidden_load(step, slot).wait()

        @pl.when(step + SLOTS - 1 < STEPS * CHUNKS)
        def _():
            hidden_load(step + SLOTS - 1, (step + SLOTS - 1) % SLOTS).start()

        def sixteen(part, carry):
            rows = pl.ds(pl.multiple_of(step * CROWS + part * 16, 16), 16)

            def store(b, block):
                normed[0, b, rows, :] = block

            norm_rows(slot, y, part, store)
            return carry

        return lax.fori_loop(0, CROWS // 16, sixteen, carry)

    with jax.named_scope("norm_shared"):
        hidden_load(tp, SLOTS).wait()

        def sixteen_shared(part, carry):
            rows = pl.ds(pl.multiple_of(part * 16, 16), 16)

            def store(b, block):
                shared[b, rows, :] = block

            norm_rows(SLOTS, 1 - y, part, store)
            return carry

        lax.fori_loop(0, CROWS // 16, sixteen_shared, 0)

    def norm_block(t, part):
        start, size = {"all": (0, 4), "0": (0, 2), "1": (2, 2)}[part]
        rows = pl.ds(pl.multiple_of(t * CROWS, CROWS), CROWS)
        return normed.at[1, pl.ds(start, size), rows, :]

    with jax.named_scope("norm"):
        lax.fori_loop(0, 4, norm_step, 0)
    with jax.named_scope("greet"):
        pl.semaphore_wait(barrier, TP - 1 + REP + 1)

    q_parts = ((0, STAGES[0][1] - HD), (STAGES[0][1] - HD, STAGES[1][1]))
    def a2a_go(stage):
        start, size = q_parts[stage]
        for d in range(1, TP):
            to = (tp + d) % TP
            there = (rep, to)
            send(
                q_weight.at[:, pl.ds(pl.multiple_of(to * QC + start, HD), size)],
                weights.at[x, my_rows, pl.ds(HD + start, size)],
                a2a_send,
                a2a_recv,
                (1 + stage) * TP + d,
                there,
            )
            if stage == 1:
                continue
            cols = pl.ds(pl.multiple_of((to // 2) * HD, HD), HD)

            def kv_copy(source, cols=cols, d=d, there=there):
                return pltpu.make_async_remote_copy(
                    src_ref=source.at[:, cols],
                    dst_ref=weights.at[x, my_rows, pl.ds(0, HD)],
                    send_sem=a2a_send.at[d],
                    recv_sem=a2a_recv.at[d],
                    device_id=there,
                    device_id_type=MESH,
                )

            from_k, from_v = kv_copy(k_weight), kv_copy(v_weight)
            pl.when(to % 2 == 0)(from_k.start)
            pl.when(to % 2 == 1)(from_v.start)
            pending.append(from_k)

    def a2a_got(stage):
        start, size = q_parts[stage]
        for d in range(1, TP):
            source = (tp + TP - d) % TP
            rows = pl.ds(pl.multiple_of(source * SHARD, SHARD), SHARD)
            receive(weights.at[x, rows, pl.ds(HD + start, size)], a2a_send, a2a_recv, (1 + stage) * TP + d)
            if stage == 0:
                receive(weights.at[x, rows, pl.ds(0, HD)], a2a_send, a2a_recv, d)

    east_dev, west_dev, y_dev = (rep_east, tp), (rep_west, tp), (rep_y, tp)

    def o_swap():
        for j in range(TP // 2):
            send(out_source(1 - y, j), out_piece(y, j), out_send, out_recv, j, y_dev)

    def o_swapped():
        for j in range(TP // 2):
            receive(out_piece(1 - y, j), out_send, out_recv, j)

    def o_own(side, base):
        block = out_block(side, x)
        send(block, block, out_send, out_recv, base, east_dev)
        send(block, block, out_send, out_recv, base + 1, west_dev)

    def o_on(side, base):
        receive(out_block(side, west), out_send, out_recv, base)
        block = out_block(side, west, "0")
        send(block, block, out_send, out_recv, base + 2, east_dev)
        receive(out_block(side, east), out_send, out_recv, base + 1)
        block = out_block(side, east, "1")
        send(block, block, out_send, out_recv, base + 3, west_dev)

    def o_far(side, base):
        receive(out_block(side, far, "0"), out_send, out_recv, base + 2)
        receive(out_block(side, far, "1"), out_send, out_recv, base + 3)

    z_up, z_down, z_far = (z + 1) % 4 * 4, (z + 3) % 4 * 4, (z + 2) % 4 * 4
    low_hi, low_core = hi_peer % 4, core_peer % 4
    low_both = low_hi + 1 - 2 * (low_hi % 2)
    up_dev, down_dev = (rep, z_up + low), (rep, z_down + low)
    hi_dev, core_dev = (rep, hi_peer), (rep, core_peer)

    class TpGather:
        def __init__(self, block, sends, recvs, base):
            self.block, self.sends, self.recvs, self.base = block, sends, recvs, base

        def go(self, k, t, to, part="all", start=True):
            block = self.block(t, part)
            return send(block, block, self.sends, self.recvs, self.base + k, to, start)

        def got(self, k, t, part="all"):
            receive(self.block(t, part), self.sends, self.recvs, self.base + k)

        def first(self, start=True):
            return [
                self.go(0, tp, hi_dev, start=start),
                self.go(1, tp, up_dev, start=start),
                self.go(2, tp, down_dev, start=start),
                self.go(3, tp, core_dev, start=start),
            ]

        def second(self):
            self.got(0, hi_peer)
            self.go(4, hi_peer, up_dev)
            self.go(5, hi_peer, down_dev)
            self.got(1, z_down + low)
            self.go(7, z_down + low, up_dev, "0")
            self.got(2, z_up + low)
            self.go(8, z_up + low, down_dev, "1")
            self.go(6, hi_peer, core_dev)
            self.go(9, z_down + low, core_dev)
            self.go(10, z_up + low, core_dev)

        def third(self):
            self.got(4, z_down + low_hi)
            self.go(11, z_down + low_hi, up_dev, "0")
            self.got(5, z_up + low_hi)
            self.go(12, z_up + low_hi, down_dev, "1")
            self.go(13, z_down + low_hi, core_dev)
            self.go(14, z_up + low_hi, core_dev)
            self.got(7, z_far + low, "0")
            self.got(8, z_far + low, "1")
            self.go(15, z_far + low, core_dev)

        def fourth(self):
            self.got(11, z_far + low_hi, "0")
            self.got(12, z_far + low_hi, "1")
            self.go(16, z_far + low_hi, core_dev)

        def near(self):
            self.got(3, core_peer)
            self.got(6, z * 4 + low_both)
            self.got(9, z_down + low_core)
            self.got(10, z_up + low_core)
            self.got(13, z_down + low_both)
            self.got(14, z_up + low_both)

        def rest(self):
            self.got(15, z_far + low_core)
            self.got(16, z_far + low_both)

    class TpGatherZ(TpGather):
        def second(self):
            self.got(1, z_down + low)
            self.go(7, z_down + low, up_dev, "0")
            self.go(4, z_down + low, hi_dev)
            self.got(2, z_up + low)
            self.go(8, z_up + low, down_dev, "1")
            self.go(5, z_up + low, hi_dev)
            self.got(0, hi_peer)
            self.go(6, hi_peer, core_dev)
            self.go(9, z_down + low, core_dev)
            self.go(10, z_up + low, core_dev)

        def third(self):
            self.got(7, z_far + low, "0")
            self.got(8, z_far + low, "1")
            self.go(11, z_far + low, hi_dev)
            self.go(15, z_far + low, core_dev)
            self.got(4, z_down + low_hi)
            self.go(13, z_down + low_hi, core_dev)
            self.got(5, z_up + low_hi)
            self.go(14, z_up + low_hi, core_dev)

        def fourth(self):
            self.got(11, z_far + low_hi)
            self.go(16, z_far + low_hi, core_dev)

    norm_gather = TpGather(norm_block, norm_send, norm_recv, 0)
    send(shared, norm_block(tp, "all"), norm_send, norm_recv, 17, y_dev)
    a2a_go(0)
    for load in out_loads:
        load.wait()
    o_own(y, 8)

    out_acc[...] = jnp.zeros_like(out_acc)

    with jax.named_scope("tables"):
        square = (ROWS, ROWS)
        rows_at = lax.broadcasted_iota(jnp.int32, square, 0)
        cols_at = lax.broadcasted_iota(jnp.int32, square, 1)

        def flip(values):
            return values.astype(jnp.float32).T.astype(jnp.int32)

        lens_col = jnp.broadcast_to(lens_row[...].astype(jnp.float32).reshape(1, ROWS), square).T
        finish_cols = jnp.broadcast_to(finish_row[...].reshape(1, ROWS), square)
        finish_rows = flip(finish_cols)
        ends[...] = finish_rows
        owner_cols = jnp.broadcast_to(owner[...].reshape(1, ROWS), square)
        owner_rows = flip(owner_cols)
        sign = jnp.where(cols_at < HD // 2, -1.0, 1.0)
        for step in range(STEPS):
            angles = (lens_col + float(step)) * frequency[...]
            cosine[pl.ds(step * ROWS, ROWS), :] = jnp.cos(angles)
            sine[pl.ds(step * ROWS, ROWS), :] = jnp.sin(angles) * sign
        same = (owner_rows == owner_cols) & (finish_rows < STEPS) & (rows_at < cols_at)
        rank = jnp.sum(jnp.where(same, 1.0, 0.0), axis=0, keepdims=True).astype(jnp.int32)
        owner_row = owner_cols[0:1, :]
        slot = (owner_row % TP) * (REP * 2) + (owner_row // TP) * 2 + rank
        slot = jnp.where(finish_cols[0:1, :] < STEPS, slot, -1)
        slots_at = lax.broadcasted_iota(jnp.int32, (REP * TP * 2, ROWS), 0)
        one_hot[...] = jnp.where(slots_at == slot, 1.0, 0.0).astype(jnp.bfloat16)
        key_at = lax.broadcasted_iota(jnp.int32, (KEYS, HD), 0)
        step_at = lax.broadcasted_iota(jnp.int32, (KEYS, HD), 1) % 8 // 2
        new_at = jnp.where(key_at - CACHE <= step_at, -1, 4 * CACHE)
        limits[...] = jnp.where(key_at < CACHE, key_at, new_at)

    def ring_block(stage, b, half):
        start, size = STAGES[stage]
        return weights.at[b, pl.ds(half * (BLOCK // 2), BLOCK // 2), pl.ds(start, size)]

    def w_go(stage, k, b, half, to):
        block = ring_block(stage, b, half)
        send(block, block, qkv_send, qkv_recv, stage * 6 + k, to)

    def w_got(stage, k, b, half):
        receive(ring_block(stage, b, half), qkv_send, qkv_recv, stage * 6 + k)

    def ring_own(stage):
        w_go(stage, 0, x, 0, east_dev)
        w_go(stage, 1, x, 1, west_dev)
        w_go(stage, 2, x, 1, east_dev)
        w_go(stage, 3, x, 0, west_dev)

    def ring_on(stage):
        w_got(stage, 0, west, 0)
        w_go(stage, 4, west, 0, east_dev)
        w_got(stage, 1, east, 1)
        w_go(stage, 5, east, 1, west_dev)

    def ring_near(stage):
        w_got(stage, 2, west, 1)
        w_got(stage, 3, east, 0)

    def ring_far(stage):
        w_got(stage, 4, far, 0)
        w_got(stage, 5, far, 1)

    def project(stage, which, b, first=False):
        start, size = STAGES[stage]

        def tile(m, carry):
            rows = pl.ds(pl.multiple_of(m * 256, 256), 256)
            part = jnp.dot(
                normed[which, b, rows, :],
                weights[b, :, start : start + size],
                preferred_element_type=jnp.float32,
            )
            if first:
                acc[which, rows, start : start + size] = part
            else:
                acc[which, rows, start : start + size] += part
            return carry

        lax.fori_loop(0, TOKENS // 256, tile, 0)

    def part_block(which, stage, half):
        start, size = STAGES[stage]
        return partial.at[which, :, pl.ds(half * HALF_ROWS, HALF_ROWS), pl.ds(start, size)]

    def part_go(stage):
        start, size = STAGES[stage]
        for half in range(2):
            for step in range(STEPS):
                rows = pl.ds(step * ROWS + half * HALF_ROWS, HALF_ROWS)
                partial[0, step, pl.ds(half * HALF_ROWS, HALF_ROWS), start : start + size] = acc[
                    1, rows, start : start + size
                ].astype(jnp.bfloat16)
            send(
                part_block(0, stage, half),
                part_block(1, stage, half),
                part_send,
                part_recv,
                stage * 2 + half,
                y_dev,
            )

    def part_got(stage, half):
        receive(part_block(1, stage, half), part_send, part_recv, stage * 2 + half)

    with jax.named_scope("norm_over_y"):
        receive(norm_block(tp, "all"), norm_send, norm_recv, 17)
        norm_gather.first()
    with jax.named_scope("a2a_wait"):
        q_load.wait()
        k_load.wait()
        a2a_got(0)
        ring_own(0)
        a2a_go(1)
    with jax.named_scope("norm"):
        lax.fori_loop(4, 16, norm_step, 0)
    with jax.named_scope("norm_second"):
        norm_gather.second()
    with jax.named_scope("ring_on_0"):
        ring_on(0)
        o_swap()
    key_load.start()
    value_load.start()
    residual_load.start()
    with jax.named_scope("norm_third"):
        norm_gather.third()
    with jax.named_scope("project"):
        project(0, 0, x, True)
    with jax.named_scope("ring_near_0"):
        ring_near(0)
    with jax.named_scope("project"):
        project(0, 0, west)
        project(0, 0, east)
    with jax.named_scope("norm_last"):
        norm_gather.fourth()
        norm_gather.near()
        norm_gather.rest()
    with jax.named_scope("project"):
        project(0, 1, x, True)
        project(0, 1, west)
        project(0, 1, east)
    with jax.named_scope("ring_far_0"):
        ring_far(0)
        a2a_got(1)
        ring_own(1)
        project(0, 1, far)
        part_go(0)
        project(0, 0, far)
    with jax.named_scope("project"):
        project(1, 0, x, True)
        project(1, 1, x, True)

    def rotate(block, rows):
        return block * cosine[rows, :] + pltpu.roll(block, HD // 2, 1) * sine[rows, :]

    def total(step, half, start):
        rows = pl.ds(step * ROWS + half * HALF_ROWS, HALF_ROWS)
        cols = slice(start, start + HD)
        there = partial[1, step, pl.ds(half * HALF_ROWS, HALF_ROWS), cols]
        return acc[0, rows, cols] + there.astype(jnp.float32)

    def place_queries(stage, half):
        for step in range(STEPS):
            rows = pl.ds(step * ROWS + half * HALF_ROWS, HALF_ROWS)
            for h in range(2):
                start = HD + (stage * 2 + h) * HD
                queries[stage, pl.ds(half * HALF_ROWS, HALF_ROWS), step * 2 + h, :] = rotate(
                    total(step, half, start), rows
                )

    is_key = tp % 2 == 0

    def pair_block(which, half):
        return pair.at[which, :, pl.ds(half * HALF_ROWS, HALF_ROWS), :]

    def pair_go(half):
        part_got(0, half)
        for step in range(STEPS):
            rows = pl.ds(step * ROWS + half * HALF_ROWS, HALF_ROWS)
            block = total(step, half, 0)
            pair[0, step, pl.ds(half * HALF_ROWS, HALF_ROWS), :] = jnp.where(
                is_key, rotate(block, rows), block
            ).astype(jnp.bfloat16)
        send(pair_block(0, half), pair_block(1, half), pair_send, pair_recv, half, core_dev)
        place_queries(0, half)

    def pair_got(half):
        receive(pair_block(1, half), pair_send, pair_recv, half)
        half_rows = pl.ds(half * HALF_ROWS, HALF_ROWS)
        for place, target in ((0, keys), (1, values)):
            spread[...] = jnp.zeros((HALF_ROWS, 16, HD), jnp.float32)
            slot = (tp + place) % 2
            for step in range(STEPS):
                spread[:, step, :] = pair[slot, step, half_rows, :].astype(jnp.float32)
            target[half_rows, pl.ds(CACHE, 16), :] = spread[...].astype(jnp.bfloat16)

    with jax.named_scope("keys"):
        pair_go(0)
    with jax.named_scope("ring_on_1"):
        ring_on(1)
    with jax.named_scope("keys"):
        key_load.wait()
        value_load.wait()
        pair_got(0)

    stays, goes = tp % 2 == y, tp % 2 != y
    row_of = lax.broadcasted_iota(jnp.int32, (KEYS, HD), 1) // 8
    score_scale = 1.0 / (float(HD) ** 0.5)

    def attend(stage, half, between):
        def rows_of_16(it, carry):
            first = half * HALF_ROWS + it * 16
            query = queries[stage, pl.ds(first, 16)].reshape(16 * 8, HD).astype(jnp.bfloat16)
            scores = None
            valid = jnp.zeros((1, HD), jnp.int32)
            for u in range(16):
                part = lax.dot_general(
                    keys[first + u], query, (((1,), (1,)), ((), ())), preferred_element_type=jnp.float32
                )
                scores = part if scores is None else jnp.where(row_of == u, part, scores)
                valid = jnp.where(row_of[0:1, :] == u, lens[first + u], valid)
            scores = jnp.where(limits[...] < valid, scores, -1e30)
            top = jnp.max(scores, axis=0, keepdims=True)
            weight = jnp.exp((scores - top) * score_scale)
            total = jnp.sum(weight, axis=0, keepdims=True)
            probs = (weight * (1.0 / total)).T
            for u in range(16):
                attn_rows[it * 16 + u] = jnp.dot(
                    probs[u * 8 : (u + 1) * 8].astype(jnp.bfloat16),
                    values[first + u],
                    preferred_element_type=jnp.float32,
                )
            return carry

        lax.fori_loop(0, HALF_ROWS // 32, rows_of_16, 0)
        between()
        lax.fori_loop(HALF_ROWS // 32, HALF_ROWS // 16, rows_of_16, 0)

        def place(target):
            for step in range(STEPS):
                for h in range(2):
                    target[
                        pl.ds(half * HALF_TOKENS + step * HALF_ROWS, HALF_ROWS),
                        pl.ds((stage * 2 + h) * HD, HD),
                    ] = attn_rows[:, step * 2 + h, :].astype(jnp.bfloat16)

        pl.when(stays)(lambda: place(gathered.at[tp]))
        pl.when(goes)(lambda: place(away))

    def attn_block(t, chunk, part="all"):
        size = HALF_TOKENS // 2
        start, size = {"all": (0, HALF_TOKENS), "0": (0, size), "1": (size, size)}[part]
        rows = pl.ds(chunk % 2 * HALF_TOKENS + start, size)
        return gathered.at[t, rows, pl.ds(chunk // 2 * 2 * HD, 2 * HD)]

    PER = 18
    gathers = [
        (TpGatherZ if chunk in Z_FIRST else TpGather)(
            lambda t, part, chunk=chunk: attn_block(t, chunk, part), attn_send, attn_recv, chunk * PER
        )
        for chunk in range(CHUNKS)
    ]

    def away_copy(chunk, to, sends, recvs, k):
        rows = pl.ds(chunk % 2 * HALF_TOKENS, HALF_TOKENS)
        return pltpu.make_async_remote_copy(
            src_ref=away.at[rows, pl.ds(chunk // 2 * 2 * HD, 2 * HD)],
            dst_ref=attn_block(core_peer, chunk),
            send_sem=sends.at[k],
            recv_sem=recvs.at[k],
            device_id=(rep_y, to),
            device_id_type=MESH,
        )

    own_sends = {}

    def attend_and_send(chunk, between=lambda: None):
        with jax.named_scope("attend"):
            attend(chunk // 2, chunk % 2, between)
        own_sends[chunk] = gathers[chunk].first(start=False)

        @pl.when(stays)
        def _():
            for copy in own_sends[chunk]:
                copy.start()

        @pl.when(goes)
        def _():
            away_copy(chunk, core_peer, away_send, away_recv, chunk).start()
            away_copy(chunk, both_peer, attn_send, attn_recv, chunk * PER).start()

    def first_of_other(chunk):
        @pl.when(goes)
        def _():
            receive(attn_block(tp, chunk), away_send, away_recv, chunk)
            for copy in own_sends[chunk][1:]:
                copy.start()

    attend_and_send(0)
    with jax.named_scope("keys"):
        pair_go(1)
    with jax.named_scope("ring_near_1"):
        ring_near(1)
        project(1, 1, west)
        project(1, 1, east)
        project(1, 0, west)
        project(1, 0, east)
    with jax.named_scope("ring_far_1"):
        ring_far(1)
        o_on(y, 8)
        o_swapped()
        o_own(1 - y, 12)
        project(1, 1, far)
        part_go(1)
        project(1, 0, far)
    with jax.named_scope("attn_0"):
        first_of_other(0)
    with jax.named_scope("keys"):
        pair_got(1)
    attend_and_send(1)
    with jax.named_scope("attn_1"):
        gathers[0].second()
    with jax.named_scope("queries"):
        for half in range(2):
            part_got(1, half)
            place_queries(1, half)

    def between_2():
        with jax.named_scope("attn_2"):
            first_of_other(1)

    attend_and_send(2, between_2)

    def between_3():
        with jax.named_scope("attn_3"):
            gathers[1].second()
            gathers[0].third()

    attend_and_send(3, between_3)
    with jax.named_scope("attn_4"):
        first_of_other(2)
        gathers[2].second()
        first_of_other(3)
        o_on(1 - y, 12)
        gathers[1].third()
        gathers[3].second()
    with jax.named_scope("attn_5"):
        gathers[0].fourth()
        gathers[2].third()
        gathers[1].fourth()
    with jax.named_scope("out_last"):
        o_far(y, 8)
        o_far(1 - y, 12)

    def out_product(half, first):
        rows = pl.ds(half * HALF_TOKENS, HALF_TOKENS)

        def step(h, carry):
            t = first + h * 2
            cols = pl.ds(pl.multiple_of((first // 2 + h) * QC, QC), QC)
            part = lax.dot_general(
                gathered[pl.ds(t, 2), rows, :].reshape(2 * HALF_TOKENS, QC),
                out_rows[:, cols],
                (((1,), (1,)), ((), ())),
                preferred_element_type=jnp.float32,
            )
            out_acc[:, rows, :] += part.reshape(2, HALF_TOKENS, QC)
            return carry

        lax.fori_loop(0, 2, step, 0)

    def out_part_go(half):
        rows = pl.ds(half * HALF_TOKENS, HALF_TOKENS)
        out_part[0, rows, :] = out_acc[1 - y, rows, :].astype(jnp.bfloat16)
        send(out_part.at[0, rows], out_part.at[1, rows], last_send, last_recv, half, y_dev)

    with jax.named_scope("attn_6"):
        gathers[0].near()
        gathers[2].near()
    with jax.named_scope("out_product"):
        out_product(0, z * 4)
        out_product(0, z_down)
        out_product(0, z_up)
    with jax.named_scope("attn_7"):
        gathers[2].fourth()
        gathers[0].rest()
        gathers[2].rest()
    with jax.named_scope("out_product"):
        out_product(0, z_far)
        out_part_go(0)
    with jax.named_scope("attn_7b"):
        gathers[3].third()
    with jax.named_scope("attn_8"):
        gathers[1].near()
        gathers[3].near()
    with jax.named_scope("out_product"):
        out_product(1, z * 4)
        out_product(1, z_down)
        out_product(1, z_up)
    with jax.named_scope("attn_9"):
        gathers[3].fourth()
        gathers[1].rest()
        gathers[3].rest()
    with jax.named_scope("out_product"):
        out_product(1, z_far)
        out_part_go(1)

    residual_load.wait()
    for half in range(2):
        rows = pl.ds(half * HALF_ROWS, HALF_ROWS)
        ended = ends[rows, 0:1]
        picked = jnp.zeros((HALF_ROWS, QC), jnp.float32)
        half_tokens = pl.ds(half * HALF_TOKENS, HALF_TOKENS)
        with jax.named_scope("out_part"):
            receive(out_part.at[1, half_tokens], last_send, last_recv, half)
        for step in range(STEPS):
            tokens = pl.ds(half * HALF_TOKENS + step * HALF_ROWS, HALF_ROWS)
            total = out_acc[y, tokens, :] + out_part[1, tokens, :].astype(jnp.float32)
            total = total + residual[step, rows, :].astype(jnp.float32)
            kept = jnp.where(ended >= step, total, 0.0).astype(jnp.bfloat16)
            decoded[step, rows, :] = kept
            picked = jnp.where(ended == step, kept.astype(jnp.float32), picked)
        at_finish[rows, :] = picked.astype(jnp.bfloat16)

    outgoing[...] = jnp.dot(
        one_hot[...], at_finish[...], preferred_element_type=jnp.float32
    ).astype(jnp.bfloat16)
    for d in range(1, TP):
        to = (tp + d) % TP
        send(
            outgoing.at[pl.ds(pl.multiple_of(to * 16, 16), 16), :],
            stage_one.at[tp],
            one_send,
            one_recv,
            d,
            (rep, to),
        )
    stage_one[tp] = outgoing[pl.ds(pl.multiple_of(tp * 16, 16), 16), :]
    with jax.named_scope("ended_one"):
        for d in range(1, TP):
            receive(stage_one.at[(tp + TP - d) % TP], one_send, one_recv, d)
    for t in range(TP):
        for part in range(QC // HD):
            arrived[:, t * 4 + part, :] = stage_one[t, :, part * HD : (part + 1) * HD].astype(jnp.float32)
    stage_two[0] = arrived[...].astype(jnp.bfloat16)
    for d in range(1, REP):
        to = (rep + d) % REP
        send(
            stage_two.at[0, pl.ds(to * 2, 2)],
            stage_two.at[1, pl.ds(rep * 2, 2)],
            two_send,
            two_recv,
            d,
            (to, tp),
        )
    stage_two[1, pl.ds(rep * 2, 2)] = stage_two[0, pl.ds(rep * 2, 2)]
    with jax.named_scope("ended_two"):
        for d in range(1, REP):
            receive(stage_two.at[1, pl.ds((rep + REP - d) % REP * 2, 2)], two_send, two_recv, d)
    for rank in range(2):
        for r in range(REP):
            arrived[rank * REP + r] = stage_two[1, r * 2 + rank].astype(jnp.float32)
    for part in range(D // HD):
        returned[:, part * HD : (part + 1) * HD] = arrived[:, part, :].astype(jnp.bfloat16)

    with jax.named_scope("sends"):
        for copy in pending:
            copy.wait_send()

        @pl.when(goes)
        def _():
            for chunk in range(CHUNKS):
                away_copy(chunk, core_peer, away_send, away_recv, chunk).wait_send()


def per_device(
    hidden,
    norm_gain,
    q_weight,
    k_weight,
    v_weight,
    o_weight,
    key_cache,
    value_cache,
    cache_len,
    finish,
    owner,
):
    half = HD // 2
    frequency = 500000.0 ** (-(np.arange(HD) % half * 2.0) / HD)
    frequency = jnp.asarray(frequency.reshape(1, HD), jnp.float32)
    hbm = pl.BlockSpec(memory_space=pl.ANY)
    vmem = pl.BlockSpec(memory_space=pltpu.VMEM)
    smem = pl.BlockSpec(memory_space=pltpu.SMEM)
    dma = pltpu.SemaphoreType.DMA
    bf16, f32 = jnp.bfloat16, jnp.float32
    return pl.pallas_call(
        kernel,
        out_shape=(
            jax.ShapeDtypeStruct((STEPS, ROWS, QC), bf16),
            jax.ShapeDtypeStruct((16, D), bf16),
        ),
        in_specs=[hbm, vmem, hbm, hbm, hbm, hbm, hbm, hbm, smem, vmem, vmem, vmem, vmem],
        out_specs=(vmem, vmem),
        scratch_shapes=[
            pltpu.VMEM((SLOTS + 1, CROWS, D), bf16),
            pltpu.VMEM((1, D), f32),
            pltpu.VMEM((4, CROWS, BLOCK), bf16),
            pltpu.VMEM((2, 4, TOKENS, BLOCK), bf16),
            pltpu.VMEM((4, BLOCK, WC), bf16),
            pltpu.VMEM((REP * SHARD, D // 2), bf16),
            pltpu.VMEM((ROWS, KEYS, HD), bf16),
            pltpu.VMEM((ROWS, KEYS, HD), bf16),
            pltpu.VMEM((2, TOKENS, WC), f32),
            pltpu.VMEM((2, ROWS, 8, HD), f32),
            pltpu.VMEM((2, STEPS, ROWS, WC), bf16),
            pltpu.VMEM((2, STEPS, ROWS, HD), bf16),
            pltpu.VMEM((HALF_ROWS, 8, HD), f32),
            pltpu.VMEM((TOKENS, QC), bf16),
            pltpu.VMEM((TP, TOKENS, QC), bf16),
            pltpu.VMEM((2, TOKENS, QC), f32),
            pltpu.VMEM((2, TOKENS, QC), bf16),
            pltpu.VMEM((STEPS, ROWS, QC), bf16),
            pltpu.VMEM((TOKENS, HD), f32),
            pltpu.VMEM((TOKENS, HD), f32),
            pltpu.VMEM((REP * TP * 2, ROWS), bf16),
            pltpu.VMEM((ROWS, ROWS), jnp.int32),
            pltpu.VMEM((KEYS, HD), jnp.int32),
            pltpu.VMEM((ROWS, QC), bf16),
            pltpu.VMEM((256, QC), bf16),
            pltpu.VMEM((TP, 16, QC), bf16),
            pltpu.VMEM((HALF_ROWS, 16, HD), f32),
            pltpu.VMEM((2, 16, D // HD, HD), bf16),
            pltpu.VMEM((16, D // HD, HD), f32),
            dma((SLOTS + 1,)),
            dma((6,)),
            dma((TP // 2,)),
            dma((3 * TP,)),
            dma((3 * TP,)),
            dma((18,)),
            dma((18,)),
            dma((12,)),
            dma((12,)),
            dma((4,)),
            dma((4,)),
            dma((18,)),
            dma((18,)),
            dma((2,)),
            dma((2,)),
            dma((CHUNKS,)),
            dma((CHUNKS,)),
            dma((18 * CHUNKS,)),
            dma((18 * CHUNKS,)),
            dma((2,)),
            dma((2,)),
            dma((TP,)),
            dma((TP,)),
            dma((REP,)),
            dma((REP,)),
        ],
        compiler_params=pltpu.CompilerParams(
            collective_id=0, has_side_effects=True, vmem_limit_bytes=60 * 1024 * 1024
        ),
    )(
        hidden,
        norm_gain,
        q_weight,
        k_weight,
        v_weight,
        o_weight,
        key_cache,
        value_cache,
        cache_len,
        cache_len,
        finish,
        owner.reshape(ROWS),
        frequency,
    )


def solution(mesh):
    placed = (
        P(None, "rep", None),
        P(),
        P(("rep", "tp"), None),
        P(("rep", "tp"), None),
        P(("rep", "tp"), None),
        P(("tp", "rep"), None),
        P("rep", "tp", None, None),
        P("rep", "tp", None, None),
        P("rep"),
        P("rep"),
        P("rep", None),
    )
    return jax.shard_map(
        per_device,
        mesh=mesh,
        in_specs=placed,
        out_specs=(P(None, "rep", "tp"), P(("rep", "tp"), None)),
        check_vma=False,
    )
```

```python
import jax
import jax.numpy as jnp
import numpy as np
from jax import lax
from jax.experimental import pallas as pl
from jax.experimental.pallas import tpu as pltpu
from jax.sharding import PartitionSpec as P

MESH = pl.DeviceIdType.MESH
KV = 8
STEPS = 4
ROWS = 128
HD = 128
CACHE = 192
KEYS = CACHE + 16
D = 8192
REP = 8
TP = 16
QC = 512
WC = QC + HD
SHARD = 64
BLOCK = TP * SHARD
TOKENS = STEPS * ROWS
CHUNKS = 4
Z_FIRST = (1,)
SLOTS = 4
CROWS = ROWS // CHUNKS
HALF_ROWS = ROWS // 2
HALF_TOKENS = HALF_ROWS * STEPS
EPS = 1e-05

STAGES = ((0, 384), (384, 256))


def kernel(
    hidden,
    gain,
    q_weight,
    k_weight,
    v_weight,
    o_weight,
    key_cache,
    value_cache,
    lens,
    lens_row,
    finish_row,
    owner,
    frequency,
    decoded,
    returned,
    staged,
    gain_row,
    shared,
    normed,
    weights,
    out_rows,
    keys,
    values,
    acc,
    queries,
    partial,
    pair,
    attn_rows,
    away,
    gathered,
    out_acc,
    out_part,
    residual,
    cosine,
    sine,
    one_hot,
    ends,
    limits,
    at_finish,
    outgoing,
    stage_one,
    spread,
    stage_two,
    arrived,
    load_sem,
    local_sem,
    out_sem,
    a2a_send,
    a2a_recv,
    norm_send,
    norm_recv,
    qkv_send,
    qkv_recv,
    part_send,
    part_recv,
    out_send,
    out_recv,
    pair_send,
    pair_recv,
    away_send,
    away_recv,
    attn_send,
    attn_recv,
    last_send,
    last_recv,
    one_send,
    one_recv,
    two_send,
    two_recv,
):
    rep = lax.axis_index("rep")
    tp = lax.axis_index("tp")
    y, x = rep // 4, rep % 4
    east, west, far = (x + 1) % 4, (x + 3) % 4, (x + 2) % 4
    rep_east, rep_west, rep_y = y * 4 + east, y * 4 + west, (1 - y) * 4 + x
    z, low = tp // 4, tp % 4
    core_peer = tp + 1 - 2 * (tp % 2)
    hi_peer = tp + 2 - 4 * ((tp // 2) % 2)
    pending = []

    def send(src, dst, sends, recvs, k, to, start=True):
        copy = pltpu.make_async_remote_copy(
            src_ref=src,
            dst_ref=dst,
            send_sem=sends.at[k],
            recv_sem=recvs.at[k],
            device_id=to,
            device_id_type=MESH,
        )
        if start:
            copy.start()
        pending.append(copy)
        return copy

    def receive(region, sends, recvs, k):
        pltpu.make_async_remote_copy(
            src_ref=region,
            dst_ref=region,
            send_sem=sends.at[k],
            recv_sem=recvs.at[k],
            device_id=(rep, core_peer),
            device_id_type=MESH,
        ).wait_recv()

    barrier = pltpu.get_barrier_semaphore()
    for d in range(1, TP):
        pl.semaphore_signal(
            barrier, inc=1, device_id=(rep, (tp + d) % TP), device_id_type=MESH
        )
    for d in range(1, REP):
        pl.semaphore_signal(
            barrier, inc=1, device_id=((rep + d) % REP, tp), device_id_type=MESH
        )
    both_peer = hi_peer + 1 - 2 * (tp % 2)
    for peer in (core_peer, both_peer):
        pl.semaphore_signal(barrier, inc=1, device_id=(rep_y, peer), device_id_type=MESH)
    key_load = pltpu.make_async_copy(
        key_cache.at[:, 0], keys.at[:, pl.ds(0, CACHE), :], local_sem.at[0]
    )
    value_load = pltpu.make_async_copy(
        value_cache.at[:, 0], values.at[:, pl.ds(0, CACHE), :], local_sem.at[1]
    )
    my_cols = pl.ds(pl.multiple_of(tp * QC, QC), QC)
    residual_load = pltpu.make_async_copy(
        hidden.at[:, :, my_cols], residual, local_sem.at[2]
    )
    my_rows = pl.ds(pl.multiple_of(tp * SHARD, SHARD), SHARD)
    q_load = pltpu.make_async_copy(
        q_weight.at[:, my_cols], weights.at[x, my_rows, pl.ds(HD, QC)], local_sem.at[3]
    )
    kv_cols = pl.ds(pl.multiple_of((tp // 2) * HD, HD), HD)
    my_kv = weights.at[x, my_rows, pl.ds(0, HD)]
    k_load = pltpu.make_async_copy(k_weight.at[:, kv_cols], my_kv, local_sem.at[4])
    v_load = pltpu.make_async_copy(v_weight.at[:, kv_cols], my_kv, local_sem.at[4])

    def out_block(side, at, part="all"):
        start, size = {"all": (0, D // 2), "0": (0, D // 4), "1": (D // 4, D // 4)}[part]
        rows = pl.ds(pl.multiple_of((side * 4 + at) * SHARD, SHARD), SHARD)
        return out_rows.at[rows, pl.ds(start, size)]

    def out_piece(side, j):
        rows = pl.ds(pl.multiple_of((side * 4 + x) * SHARD, SHARD), SHARD)
        return out_rows.at[rows, pl.ds(j * QC, QC)]

    def out_source(core, j):
        return o_weight.at[:, pl.ds(pl.multiple_of((j * 2 + core) * QC, QC), QC)]

    out_loads = [
        pltpu.make_async_copy(out_source(y, j), out_piece(y, j), out_sem.at[j]) for j in range(TP // 2)
    ]
    q_load.start()
    pl.when(tp % 2 == 0)(k_load.start)
    pl.when(tp % 2 == 1)(v_load.start)
    for load in out_loads:
        load.start()

    def hidden_load(step, slot):
        return pltpu.make_async_copy(
            hidden.at[step // CHUNKS, pl.ds(pl.multiple_of((step % CHUNKS) * CROWS, CROWS), CROWS), :],
            staged.at[slot],
            load_sem.at[slot],
        )

    hidden_load(tp, SLOTS).start()
    gain_row[...] = gain[...].astype(jnp.float32).reshape(1, D)
    for step in range(SLOTS - 1):
        hidden_load(step, step).start()
    def norm_rows(slot, half, part, store):
        part_rows = pl.ds(pl.multiple_of(part * 16, 16), 16)
        values_f = staged[slot, part_rows, :].astype(jnp.float32)
        mean = jnp.mean(values_f * values_f, axis=-1, keepdims=True)
        scale = lax.rsqrt(mean + EPS)
        for b in range(4):
            cols = pl.ds(pl.multiple_of(half * (D // 2) + b * BLOCK, BLOCK), BLOCK)
            block = staged[slot, part_rows, cols].astype(jnp.float32)
            block = block * scale * gain_row[:, cols]
            store(b, block.astype(jnp.bfloat16))

    def norm_step(step, carry):
        slot = step % SLOTS
        hidden_load(step, slot).wait()

        @pl.when(step + SLOTS - 1 < STEPS * CHUNKS)
        def _():
            hidden_load(step + SLOTS - 1, (step + SLOTS - 1) % SLOTS).start()

        def sixteen(part, carry):
            rows = pl.ds(pl.multiple_of(step * CROWS + part * 16, 16), 16)

            def store(b, block):
                normed[0, b, rows, :] = block

            norm_rows(slot, y, part, store)
            return carry

        return lax.fori_loop(0, CROWS // 16, sixteen, carry)

    with jax.named_scope("norm_shared"):
        hidden_load(tp, SLOTS).wait()

        def sixteen_shared(part, carry):
            rows = pl.ds(pl.multiple_of(part * 16, 16), 16)

            def store(b, block):
                shared[b, rows, :] = block

            norm_rows(SLOTS, 1 - y, part, store)
            return carry

        lax.fori_loop(0, CROWS // 16, sixteen_shared, 0)

    def norm_block(t, part):
        start, size = {"all": (0, 4), "0": (0, 2), "1": (2, 2)}[part]
        rows = pl.ds(pl.multiple_of(t * CROWS, CROWS), CROWS)
        return normed.at[1, pl.ds(start, size), rows, :]

    with jax.named_scope("norm"):
        lax.fori_loop(0, 4, norm_step, 0)
    with jax.named_scope("greet"):
        pl.semaphore_wait(barrier, TP - 1 + REP + 1)

    q_parts = ((0, STAGES[0][1] - HD), (STAGES[0][1] - HD, STAGES[1][1]))
    def a2a_go(stage):
        start, size = q_parts[stage]
        for d in range(1, TP):
            to = (tp + d) % TP
            there = (rep, to)
            send(
                q_weight.at[:, pl.ds(pl.multiple_of(to * QC + start, HD), size)],
                weights.at[x, my_rows, pl.ds(HD + start, size)],
                a2a_send,
                a2a_recv,
                (1 + stage) * TP + d,
                there,
            )
            if stage == 1:
                continue
            cols = pl.ds(pl.multiple_of((to // 2) * HD, HD), HD)

            def kv_copy(source, cols=cols, d=d, there=there):
                return pltpu.make_async_remote_copy(
                    src_ref=source.at[:, cols],
                    dst_ref=weights.at[x, my_rows, pl.ds(0, HD)],
                    send_sem=a2a_send.at[d],
                    recv_sem=a2a_recv.at[d],
                    device_id=there,
                    device_id_type=MESH,
                )

            from_k, from_v = kv_copy(k_weight), kv_copy(v_weight)
            pl.when(to % 2 == 0)(from_k.start)
            pl.when(to % 2 == 1)(from_v.start)
            pending.append(from_k)

    def a2a_got(stage):
        start, size = q_parts[stage]
        for d in range(1, TP):
            source = (tp + TP - d) % TP
            rows = pl.ds(pl.multiple_of(source * SHARD, SHARD), SHARD)
            receive(weights.at[x, rows, pl.ds(HD + start, size)], a2a_send, a2a_recv, (1 + stage) * TP + d)
            if stage == 0:
                receive(weights.at[x, rows, pl.ds(0, HD)], a2a_send, a2a_recv, d)

    east_dev, west_dev, y_dev = (rep_east, tp), (rep_west, tp), (rep_y, tp)

    def o_swap():
        for j in range(TP // 2):
            send(out_source(1 - y, j), out_piece(y, j), out_send, out_recv, j, y_dev)

    def o_swapped():
        for j in range(TP // 2):
            receive(out_piece(1 - y, j), out_send, out_recv, j)

    def o_own(side, base):
        block = out_block(side, x)
        send(block, block, out_send, out_recv, base, east_dev)
        send(block, block, out_send, out_recv, base + 1, west_dev)

    def o_on(side, base):
        receive(out_block(side, west), out_send, out_recv, base)
        block = out_block(side, west, "0")
        send(block, block, out_send, out_recv, base + 2, east_dev)
        receive(out_block(side, east), out_send, out_recv, base + 1)
        block = out_block(side, east, "1")
        send(block, block, out_send, out_recv, base + 3, west_dev)

    def o_far(side, base):
        receive(out_block(side, far, "0"), out_send, out_recv, base + 2)
        receive(out_block(side, far, "1"), out_send, out_recv, base + 3)

    z_up, z_down, z_far = (z + 1) % 4 * 4, (z + 3) % 4 * 4, (z + 2) % 4 * 4
    low_hi, low_core = hi_peer % 4, core_peer % 4
    low_both = low_hi + 1 - 2 * (low_hi % 2)
    up_dev, down_dev = (rep, z_up + low), (rep, z_down + low)
    hi_dev, core_dev = (rep, hi_peer), (rep, core_peer)

    class TpGather:
        def __init__(self, block, sends, recvs, base):
            self.block, self.sends, self.recvs, self.base = block, sends, recvs, base

        def go(self, k, t, to, part="all", start=True):
            block = self.block(t, part)
            return send(block, block, self.sends, self.recvs, self.base + k, to, start)

        def got(self, k, t, part="all"):
            receive(self.block(t, part), self.sends, self.recvs, self.base + k)

        def first(self, start=True):
            return [
                self.go(0, tp, hi_dev, start=start),
                self.go(1, tp, up_dev, start=start),
                self.go(2, tp, down_dev, start=start),
                self.go(3, tp, core_dev, start=start),
            ]

        def second(self):
            self.got(0, hi_peer)
            self.go(4, hi_peer, up_dev)
            self.go(5, hi_peer, down_dev)
            self.got(1, z_down + low)
            self.go(7, z_down + low, up_dev, "0")
            self.got(2, z_up + low)
            self.go(8, z_up + low, down_dev, "1")
            self.go(6, hi_peer, core_dev)
            self.go(9, z_down + low, core_dev)
            self.go(10, z_up + low, core_dev)

        def third(self):
            self.got(4, z_down + low_hi)
            self.go(11, z_down + low_hi, up_dev, "0")
            self.got(5, z_up + low_hi)
            self.go(12, z_up + low_hi, down_dev, "1")
            self.go(13, z_down + low_hi, core_dev)
            self.go(14, z_up + low_hi, core_dev)
            self.got(7, z_far + low, "0")
            self.got(8, z_far + low, "1")
            self.go(15, z_far + low, core_dev)

        def fourth(self):
            self.got(11, z_far + low_hi, "0")
            self.got(12, z_far + low_hi, "1")
            self.go(16, z_far + low_hi, core_dev)

        def near(self):
            self.got(3, core_peer)
            self.got(6, z * 4 + low_both)
            self.got(9, z_down + low_core)
            self.got(10, z_up + low_core)
            self.got(13, z_down + low_both)
            self.got(14, z_up + low_both)

        def rest(self):
            self.got(15, z_far + low_core)
            self.got(16, z_far + low_both)

    class TpGatherZ(TpGather):
        def second(self):
            self.got(1, z_down + low)
            self.go(7, z_down + low, up_dev, "0")
            self.go(4, z_down + low, hi_dev)
            self.got(2, z_up + low)
            self.go(8, z_up + low, down_dev, "1")
            self.go(5, z_up + low, hi_dev)
            self.got(0, hi_peer)
            self.go(6, hi_peer, core_dev)
            self.go(9, z_down + low, core_dev)
            self.go(10, z_up + low, core_dev)

        def third(self):
            self.got(7, z_far + low, "0")
            self.got(8, z_far + low, "1")
            self.go(11, z_far + low, hi_dev)
            self.go(15, z_far + low, core_dev)
            self.got(4, z_down + low_hi)
            self.go(13, z_down + low_hi, core_dev)
            self.got(5, z_up + low_hi)
            self.go(14, z_up + low_hi, core_dev)

        def fourth(self):
            self.got(11, z_far + low_hi)
            self.go(16, z_far + low_hi, core_dev)

    norm_gather = TpGather(norm_block, norm_send, norm_recv, 0)
    send(shared, norm_block(tp, "all"), norm_send, norm_recv, 17, y_dev)
    a2a_go(0)
    for load in out_loads:
        load.wait()
    o_own(y, 8)

    out_acc[...] = jnp.zeros_like(out_acc)

    with jax.named_scope("tables"):
        square = (ROWS, ROWS)
        rows_at = lax.broadcasted_iota(jnp.int32, square, 0)
        cols_at = lax.broadcasted_iota(jnp.int32, square, 1)

        def flip(values):
            return values.astype(jnp.float32).T.astype(jnp.int32)

        lens_col = jnp.broadcast_to(lens_row[...].astype(jnp.float32).reshape(1, ROWS), square).T
        finish_cols = jnp.broadcast_to(finish_row[...].reshape(1, ROWS), square)
        finish_rows = flip(finish_cols)
        ends[...] = finish_rows
        owner_cols = jnp.broadcast_to(owner[...].reshape(1, ROWS), square)
        owner_rows = flip(owner_cols)
        sign = jnp.where(cols_at < HD // 2, -1.0, 1.0)
        for step in range(STEPS):
            angles = (lens_col + float(step)) * frequency[...]
            cosine[pl.ds(step * ROWS, ROWS), :] = jnp.cos(angles)
            sine[pl.ds(step * ROWS, ROWS), :] = jnp.sin(angles) * sign
        same = (owner_rows == owner_cols) & (finish_rows < STEPS) & (rows_at < cols_at)
        rank = jnp.sum(jnp.where(same, 1.0, 0.0), axis=0, keepdims=True).astype(jnp.int32)
        owner_row = owner_cols[0:1, :]
        slot = (owner_row % TP) * (REP * 2) + (owner_row // TP) * 2 + rank
        slot = jnp.where(finish_cols[0:1, :] < STEPS, slot, -1)
        slots_at = lax.broadcasted_iota(jnp.int32, (REP * TP * 2, ROWS), 0)
        one_hot[...] = jnp.where(slots_at == slot, 1.0, 0.0).astype(jnp.bfloat16)
        key_at = lax.broadcasted_iota(jnp.int32, (KEYS, HD), 0)
        step_at = lax.broadcasted_iota(jnp.int32, (KEYS, HD), 1) % 8 // 2
        new_at = jnp.where(key_at - CACHE <= step_at, -1, 4 * CACHE)
        limits[...] = jnp.where(key_at < CACHE, key_at, new_at)

    def ring_block(stage, b, half):
        start, size = STAGES[stage]
        return weights.at[b, pl.ds(half * (BLOCK // 2), BLOCK // 2), pl.ds(start, size)]

    def w_go(stage, k, b, half, to):
        block = ring_block(stage, b, half)
        send(block, block, qkv_send, qkv_recv, stage * 6 + k, to)

    def w_got(stage, k, b, half):
        receive(ring_block(stage, b, half), qkv_send, qkv_recv, stage * 6 + k)

    def ring_own(stage):
        w_go(stage, 0, x, 0, east_dev)
        w_go(stage, 1, x, 1, west_dev)
        w_go(stage, 2, x, 1, east_dev)
        w_go(stage, 3, x, 0, west_dev)

    def ring_on(stage):
        w_got(stage, 0, west, 0)
        w_go(stage, 4, west, 0, east_dev)
        w_got(stage, 1, east, 1)
        w_go(stage, 5, east, 1, west_dev)

    def ring_near(stage):
        w_got(stage, 2, west, 1)
        w_got(stage, 3, east, 0)

    def ring_far(stage):
        w_got(stage, 4, far, 0)
        w_got(stage, 5, far, 1)

    def project(stage, which, b, first=False):
        start, size = STAGES[stage]

        def tile(m, carry):
            rows = pl.ds(pl.multiple_of(m * 256, 256), 256)
            part = jnp.dot(
                normed[which, b, rows, :],
                weights[b, :, start : start + size],
                preferred_element_type=jnp.float32,
            )
            if first:
                acc[which, rows, start : start + size] = part
            else:
                acc[which, rows, start : start + size] += part
            return carry

        lax.fori_loop(0, TOKENS // 256, tile, 0)

    def part_block(which, stage, half):
        start, size = STAGES[stage]
        return partial.at[which, :, pl.ds(half * HALF_ROWS, HALF_ROWS), pl.ds(start, size)]

    def part_go(stage, half):
        start, size = STAGES[stage]
        for step in range(STEPS):
            rows = pl.ds(step * ROWS + half * HALF_ROWS, HALF_ROWS)
            partial[0, step, pl.ds(half * HALF_ROWS, HALF_ROWS), start : start + size] = acc[
                1, rows, start : start + size
            ].astype(jnp.bfloat16)
        send(
            part_block(0, stage, half),
            part_block(1, stage, half),
            part_send,
            part_recv,
            stage * 2 + half,
            y_dev,
        )

    def part_got(stage, half):
        receive(part_block(1, stage, half), part_send, part_recv, stage * 2 + half)

    with jax.named_scope("norm_over_y"):
        receive(norm_block(tp, "all"), norm_send, norm_recv, 17)
        norm_gather.first()
    with jax.named_scope("a2a_wait"):
        q_load.wait()
        k_load.wait()
        a2a_got(0)
        ring_own(0)
        a2a_go(1)
    with jax.named_scope("norm"):
        lax.fori_loop(4, 16, norm_step, 0)
    with jax.named_scope("norm_second"):
        norm_gather.second()
    with jax.named_scope("ring_on_0"):
        ring_on(0)
        o_swap()
    key_load.start()
    value_load.start()
    residual_load.start()
    with jax.named_scope("norm_third"):
        norm_gather.third()
    with jax.named_scope("project"):
        project(0, 0, x, True)
    with jax.named_scope("ring_near_0"):
        ring_near(0)
    with jax.named_scope("project"):
        project(0, 0, west)
        project(0, 0, east)
    with jax.named_scope("norm_last"):
        norm_gather.fourth()
        norm_gather.near()
        norm_gather.rest()
    with jax.named_scope("project"):
        project(0, 1, x, True)
        project(0, 1, west)
        project(0, 1, east)
    with jax.named_scope("ring_far_0"):
        ring_far(0)
        a2a_got(1)
        ring_own(1)
        project(0, 1, far)
        part_go(0, 0)
        project(0, 0, far)
    with jax.named_scope("project"):
        project(1, 0, x, True)
        project(1, 1, x, True)
        part_go(0, 1)

    def rotate(block, rows):
        return block * cosine[rows, :] + pltpu.roll(block, HD // 2, 1) * sine[rows, :]

    def total(step, half, start):
        rows = pl.ds(step * ROWS + half * HALF_ROWS, HALF_ROWS)
        cols = slice(start, start + HD)
        there = partial[1, step, pl.ds(half * HALF_ROWS, HALF_ROWS), cols]
        return acc[0, rows, cols] + there.astype(jnp.float32)

    def place_queries(stage, half):
        for step in range(STEPS):
            rows = pl.ds(step * ROWS + half * HALF_ROWS, HALF_ROWS)
            for h in range(2):
                start = HD + (stage * 2 + h) * HD
                queries[stage, pl.ds(half * HALF_ROWS, HALF_ROWS), step * 2 + h, :] = rotate(
                    total(step, half, start), rows
                )

    is_key = tp % 2 == 0

    def pair_block(which, half):
        return pair.at[which, :, pl.ds(half * HALF_ROWS, HALF_ROWS), :]

    def pair_go(half):
        part_got(0, half)
        for step in range(STEPS):
            rows = pl.ds(step * ROWS + half * HALF_ROWS, HALF_ROWS)
            block = total(step, half, 0)
            pair[0, step, pl.ds(half * HALF_ROWS, HALF_ROWS), :] = jnp.where(
                is_key, rotate(block, rows), block
            ).astype(jnp.bfloat16)
        send(pair_block(0, half), pair_block(1, half), pair_send, pair_recv, half, core_dev)
        place_queries(0, half)

    def pair_got(half):
        receive(pair_block(1, half), pair_send, pair_recv, half)
        half_rows = pl.ds(half * HALF_ROWS, HALF_ROWS)
        for place, target in ((0, keys), (1, values)):
            spread[...] = jnp.zeros((HALF_ROWS, 16, HD), jnp.float32)
            slot = (tp + place) % 2
            for step in range(STEPS):
                spread[:, step, :] = pair[slot, step, half_rows, :].astype(jnp.float32)
            target[half_rows, pl.ds(CACHE, 16), :] = spread[...].astype(jnp.bfloat16)

    with jax.named_scope("keys"):
        pair_go(0)
    with jax.named_scope("ring_on_1"):
        ring_on(1)
    with jax.named_scope("keys"):
        key_load.wait()
        value_load.wait()
        pair_got(0)

    stays, goes = tp % 2 == y, tp % 2 != y
    row_of = lax.broadcasted_iota(jnp.int32, (KEYS, HD), 1) // 8
    score_scale = 1.0 / (float(HD) ** 0.5)

    def attend(stage, half, between):
        def rows_of_16(it, carry):
            first = half * HALF_ROWS + it * 16
            query = queries[stage, pl.ds(first, 16)].reshape(16 * 8, HD).astype(jnp.bfloat16)
            scores = None
            valid = jnp.zeros((1, HD), jnp.int32)
            for u in range(16):
                part = lax.dot_general(
                    keys[first + u], query, (((1,), (1,)), ((), ())), preferred_element_type=jnp.float32
                )
                scores = part if scores is None else jnp.where(row_of == u, part, scores)
                valid = jnp.where(row_of[0:1, :] == u, lens[first + u], valid)
            scores = jnp.where(limits[...] < valid, scores, -1e30)
            top = jnp.max(scores, axis=0, keepdims=True)
            weight = jnp.exp((scores - top) * score_scale)
            total = jnp.sum(weight, axis=0, keepdims=True)
            probs = (weight * (1.0 / total)).T
            for u in range(16):
                attn_rows[it * 16 + u] = jnp.dot(
                    probs[u * 8 : (u + 1) * 8].astype(jnp.bfloat16),
                    values[first + u],
                    preferred_element_type=jnp.float32,
                )
            return carry

        lax.fori_loop(0, HALF_ROWS // 32, rows_of_16, 0)
        between()
        lax.fori_loop(HALF_ROWS // 32, HALF_ROWS // 16, rows_of_16, 0)

        def place(target):
            for step in range(STEPS):
                for h in range(2):
                    target[
                        pl.ds(half * HALF_TOKENS + step * HALF_ROWS, HALF_ROWS),
                        pl.ds((stage * 2 + h) * HD, HD),
                    ] = attn_rows[:, step * 2 + h, :].astype(jnp.bfloat16)

        pl.when(stays)(lambda: place(gathered.at[tp]))
        pl.when(goes)(lambda: place(away))

    def attn_block(t, chunk, part="all"):
        size = HALF_TOKENS // 2
        start, size = {"all": (0, HALF_TOKENS), "0": (0, size), "1": (size, size)}[part]
        rows = pl.ds(chunk % 2 * HALF_TOKENS + start, size)
        return gathered.at[t, rows, pl.ds(chunk // 2 * 2 * HD, 2 * HD)]

    PER = 18
    gathers = [
        (TpGatherZ if chunk in Z_FIRST else TpGather)(
            lambda t, part, chunk=chunk: attn_block(t, chunk, part), attn_send, attn_recv, chunk * PER
        )
        for chunk in range(CHUNKS)
    ]

    def away_copy(chunk, to, sends, recvs, k):
        rows = pl.ds(chunk % 2 * HALF_TOKENS, HALF_TOKENS)
        return pltpu.make_async_remote_copy(
            src_ref=away.at[rows, pl.ds(chunk // 2 * 2 * HD, 2 * HD)],
            dst_ref=attn_block(core_peer, chunk),
            send_sem=sends.at[k],
            recv_sem=recvs.at[k],
            device_id=(rep_y, to),
            device_id_type=MESH,
        )

    own_sends = {}

    def attend_and_send(chunk, between=lambda: None):
        with jax.named_scope("attend"):
            attend(chunk // 2, chunk % 2, between)
        own_sends[chunk] = gathers[chunk].first(start=False)

        @pl.when(stays)
        def _():
            for copy in own_sends[chunk]:
                copy.start()

        @pl.when(goes)
        def _():
            away_copy(chunk, core_peer, away_send, away_recv, chunk).start()
            away_copy(chunk, both_peer, attn_send, attn_recv, chunk * PER).start()

    def first_of_other(chunk):
        @pl.when(goes)
        def _():
            receive(attn_block(tp, chunk), away_send, away_recv, chunk)
            for copy in own_sends[chunk][1:]:
                copy.start()

    attend_and_send(0)
    with jax.named_scope("keys"):
        pair_go(1)
    with jax.named_scope("ring_near_1"):
        ring_near(1)
        project(1, 1, west)
        project(1, 1, east)
    with jax.named_scope("ring_far_1"):
        ring_far(1)
        project(1, 1, far)
        part_go(1, 0)
        o_on(y, 8)
        o_swapped()
        o_own(1 - y, 12)
    with jax.named_scope("attn_0"):
        first_of_other(0)
    with jax.named_scope("keys"):
        pair_got(1)
    attend_and_send(1, lambda: part_go(1, 1))
    with jax.named_scope("attn_1"):
        gathers[0].second()
    with jax.named_scope("project"):
        project(1, 0, west)
        project(1, 0, east)
        project(1, 0, far)
    with jax.named_scope("queries"):
        part_got(1, 0)
        place_queries(1, 0)

    def between_2():
        with jax.named_scope("attn_2"):
            first_of_other(1)

    attend_and_send(2, between_2)
    with jax.named_scope("queries"):
        part_got(1, 1)
        place_queries(1, 1)

    def between_3():
        with jax.named_scope("attn_3"):
            gathers[1].second()
            gathers[0].third()

    attend_and_send(3, between_3)
    with jax.named_scope("attn_4"):
        first_of_other(2)
        gathers[2].second()
        first_of_other(3)
        o_on(1 - y, 12)
        gathers[1].third()
        gathers[3].second()
    with jax.named_scope("attn_5"):
        gathers[0].fourth()
        gathers[2].third()
        gathers[1].fourth()
    with jax.named_scope("out_last"):
        o_far(y, 8)
        o_far(1 - y, 12)

    def out_product(half, first):
        rows = pl.ds(half * HALF_TOKENS, HALF_TOKENS)

        def step(h, carry):
            t = first + h * 2
            cols = pl.ds(pl.multiple_of((first // 2 + h) * QC, QC), QC)
            part = lax.dot_general(
                gathered[pl.ds(t, 2), rows, :].reshape(2 * HALF_TOKENS, QC),
                out_rows[:, cols],
                (((1,), (1,)), ((), ())),
                preferred_element_type=jnp.float32,
            )
            out_acc[:, rows, :] += part.reshape(2, HALF_TOKENS, QC)
            return carry

        lax.fori_loop(0, 2, step, 0)

    def out_part_go(half):
        rows = pl.ds(half * HALF_TOKENS, HALF_TOKENS)
        out_part[0, rows, :] = out_acc[1 - y, rows, :].astype(jnp.bfloat16)
        send(out_part.at[0, rows], out_part.at[1, rows], last_send, last_recv, half, y_dev)

    with jax.named_scope("attn_6"):
        gathers[0].near()
        gathers[2].near()
    with jax.named_scope("out_product"):
        out_product(0, z * 4)
        out_product(0, z_down)
        out_product(0, z_up)
    with jax.named_scope("attn_7"):
        gathers[2].fourth()
        gathers[0].rest()
        gathers[2].rest()
    with jax.named_scope("out_product"):
        out_product(0, z_far)
        out_part_go(0)
    with jax.named_scope("attn_7b"):
        gathers[3].third()
    with jax.named_scope("attn_8"):
        gathers[1].near()
        gathers[3].near()
    with jax.named_scope("out_product"):
        out_product(1, z * 4)
        out_product(1, z_down)
        out_product(1, z_up)
    with jax.named_scope("attn_9"):
        gathers[3].fourth()
        gathers[1].rest()
        gathers[3].rest()
    with jax.named_scope("out_product"):
        out_product(1, z_far)
        out_part_go(1)

    residual_load.wait()
    for half in range(2):
        rows = pl.ds(half * HALF_ROWS, HALF_ROWS)
        ended = ends[rows, 0:1]
        picked = jnp.zeros((HALF_ROWS, QC), jnp.float32)
        half_tokens = pl.ds(half * HALF_TOKENS, HALF_TOKENS)
        with jax.named_scope("out_part"):
            receive(out_part.at[1, half_tokens], last_send, last_recv, half)
        for step in range(STEPS):
            tokens = pl.ds(half * HALF_TOKENS + step * HALF_ROWS, HALF_ROWS)
            total = out_acc[y, tokens, :] + out_part[1, tokens, :].astype(jnp.float32)
            total = total + residual[step, rows, :].astype(jnp.float32)
            kept = jnp.where(ended >= step, total, 0.0).astype(jnp.bfloat16)
            decoded[step, rows, :] = kept
            picked = jnp.where(ended == step, kept.astype(jnp.float32), picked)
        at_finish[rows, :] = picked.astype(jnp.bfloat16)

    outgoing[...] = jnp.dot(
        one_hot[...], at_finish[...], preferred_element_type=jnp.float32
    ).astype(jnp.bfloat16)
    for d in range(1, TP):
        to = (tp + d) % TP
        send(
            outgoing.at[pl.ds(pl.multiple_of(to * 16, 16), 16), :],
            stage_one.at[tp],
            one_send,
            one_recv,
            d,
            (rep, to),
        )
    stage_one[tp] = outgoing[pl.ds(pl.multiple_of(tp * 16, 16), 16), :]
    with jax.named_scope("ended_one"):
        for d in range(1, TP):
            receive(stage_one.at[(tp + TP - d) % TP], one_send, one_recv, d)
    for t in range(TP):
        for part in range(QC // HD):
            arrived[:, t * 4 + part, :] = stage_one[t, :, part * HD : (part + 1) * HD].astype(jnp.float32)
    stage_two[0] = arrived[...].astype(jnp.bfloat16)
    for d in range(1, REP):
        to = (rep + d) % REP
        send(
            stage_two.at[0, pl.ds(to * 2, 2)],
            stage_two.at[1, pl.ds(rep * 2, 2)],
            two_send,
            two_recv,
            d,
            (to, tp),
        )
    stage_two[1, pl.ds(rep * 2, 2)] = stage_two[0, pl.ds(rep * 2, 2)]
    with jax.named_scope("ended_two"):
        for d in range(1, REP):
            receive(stage_two.at[1, pl.ds((rep + REP - d) % REP * 2, 2)], two_send, two_recv, d)
    for rank in range(2):
        for r in range(REP):
            arrived[rank * REP + r] = stage_two[1, r * 2 + rank].astype(jnp.float32)
    for part in range(D // HD):
        returned[:, part * HD : (part + 1) * HD] = arrived[:, part, :].astype(jnp.bfloat16)

    with jax.named_scope("sends"):
        for copy in pending:
            copy.wait_send()

        @pl.when(goes)
        def _():
            for chunk in range(CHUNKS):
                away_copy(chunk, core_peer, away_send, away_recv, chunk).wait_send()


def per_device(
    hidden,
    norm_gain,
    q_weight,
    k_weight,
    v_weight,
    o_weight,
    key_cache,
    value_cache,
    cache_len,
    finish,
    owner,
):
    half = HD // 2
    frequency = 500000.0 ** (-(np.arange(HD) % half * 2.0) / HD)
    frequency = jnp.asarray(frequency.reshape(1, HD), jnp.float32)
    hbm = pl.BlockSpec(memory_space=pl.ANY)
    vmem = pl.BlockSpec(memory_space=pltpu.VMEM)
    smem = pl.BlockSpec(memory_space=pltpu.SMEM)
    dma = pltpu.SemaphoreType.DMA
    bf16, f32 = jnp.bfloat16, jnp.float32
    return pl.pallas_call(
        kernel,
        out_shape=(
            jax.ShapeDtypeStruct((STEPS, ROWS, QC), bf16),
            jax.ShapeDtypeStruct((16, D), bf16),
        ),
        in_specs=[hbm, vmem, hbm, hbm, hbm, hbm, hbm, hbm, smem, vmem, vmem, vmem, vmem],
        out_specs=(vmem, vmem),
        scratch_shapes=[
            pltpu.VMEM((SLOTS + 1, CROWS, D), bf16),
            pltpu.VMEM((1, D), f32),
            pltpu.VMEM((4, CROWS, BLOCK), bf16),
            pltpu.VMEM((2, 4, TOKENS, BLOCK), bf16),
            pltpu.VMEM((4, BLOCK, WC), bf16),
            pltpu.VMEM((REP * SHARD, D // 2), bf16),
            pltpu.VMEM((ROWS, KEYS, HD), bf16),
            pltpu.VMEM((ROWS, KEYS, HD), bf16),
            pltpu.VMEM((2, TOKENS, WC), f32),
            pltpu.VMEM((2, ROWS, 8, HD), f32),
            pltpu.VMEM((2, STEPS, ROWS, WC), bf16),
            pltpu.VMEM((2, STEPS, ROWS, HD), bf16),
            pltpu.VMEM((HALF_ROWS, 8, HD), f32),
            pltpu.VMEM((TOKENS, QC), bf16),
            pltpu.VMEM((TP, TOKENS, QC), bf16),
            pltpu.VMEM((2, TOKENS, QC), f32),
            pltpu.VMEM((2, TOKENS, QC), bf16),
            pltpu.VMEM((STEPS, ROWS, QC), bf16),
            pltpu.VMEM((TOKENS, HD), f32),
            pltpu.VMEM((TOKENS, HD), f32),
            pltpu.VMEM((REP * TP * 2, ROWS), bf16),
            pltpu.VMEM((ROWS, ROWS), jnp.int32),
            pltpu.VMEM((KEYS, HD), jnp.int32),
            pltpu.VMEM((ROWS, QC), bf16),
            pltpu.VMEM((256, QC), bf16),
            pltpu.VMEM((TP, 16, QC), bf16),
            pltpu.VMEM((HALF_ROWS, 16, HD), f32),
            pltpu.VMEM((2, 16, D // HD, HD), bf16),
            pltpu.VMEM((16, D // HD, HD), f32),
            dma((SLOTS + 1,)),
            dma((6,)),
            dma((TP // 2,)),
            dma((3 * TP,)),
            dma((3 * TP,)),
            dma((18,)),
            dma((18,)),
            dma((12,)),
            dma((12,)),
            dma((4,)),
            dma((4,)),
            dma((18,)),
            dma((18,)),
            dma((2,)),
            dma((2,)),
            dma((CHUNKS,)),
            dma((CHUNKS,)),
            dma((18 * CHUNKS,)),
            dma((18 * CHUNKS,)),
            dma((2,)),
            dma((2,)),
            dma((TP,)),
            dma((TP,)),
            dma((REP,)),
            dma((REP,)),
        ],
        compiler_params=pltpu.CompilerParams(
            collective_id=0, has_side_effects=True, vmem_limit_bytes=60 * 1024 * 1024
        ),
    )(
        hidden,
        norm_gain,
        q_weight,
        k_weight,
        v_weight,
        o_weight,
        key_cache,
        value_cache,
        cache_len,
        cache_len,
        finish,
        owner.reshape(ROWS),
        frequency,
    )


def solution(mesh):
    placed = (
        P(None, "rep", None),
        P(),
        P(("rep", "tp"), None),
        P(("rep", "tp"), None),
        P(("rep", "tp"), None),
        P(("tp", "rep"), None),
        P("rep", "tp", None, None),
        P("rep", "tp", None, None),
        P("rep"),
        P("rep"),
        P("rep", None),
    )
    return jax.shard_map(
        per_device,
        mesh=mesh,
        in_specs=placed,
        out_specs=(P(None, "rep", "tp"), P(("rep", "tp"), None)),
        check_vma=False,
    )
```
